32 devices in a mesh: fsdp: 32 (over z, y, x, core).
Axes of the slice: x: 2, y: 2, z: 4, core: 2. Of those that a mesh axis runs over, the one named last changes fastest.
Arguments:
- block_input: bfloat16 [8192, 2048], P('fsdp'), may hold values from -6 to 6
- cotangent: bfloat16 [8192, 2048], P('fsdp'), may hold values from -6 to 6
- inward_weight: float32 [2048, 6144], P('fsdp'), may hold values from -0.125 to 0.125
- inward_first: float32 [2048, 6144], P('fsdp'), may hold values from -80 to 80
- inward_second: float32 [2048, 6144], P('fsdp'), may hold values from 729.088 to 2916.352
- outward_weight: float32 [2048, 2048], P('fsdp'), may hold values from -0.125 to 0.125
- outward_first: float32 [2048, 2048], P('fsdp'), may hold values from -80 to 80
- outward_second: float32 [2048, 2048], P('fsdp'), may hold values from 729.088 to 2916.352
- gate_weight: float32 [2048, 8192], P('fsdp'), may hold values from -0.125 to 0.125
- gate_first: float32 [2048, 8192], P('fsdp'), may hold values from -16 to 16
- gate_second: float32 [2048, 8192], P('fsdp'), may hold values from 38.5024 to 155.648
- up_weight: float32 [2048, 8192], P('fsdp'), may hold values from -0.125 to 0.125
- up_first: float32 [2048, 8192], P('fsdp'), may hold values from -16 to 16
- up_second: float32 [2048, 8192], P('fsdp'), may hold values from 38.5024 to 155.648
- down_weight: float32 [8192, 2048], P('fsdp'), may hold values from -0.0625 to 0.0625
- down_first: float32 [8192, 2048], P('fsdp'), may hold values from -32 to 32
- down_second: float32 [8192, 2048], P('fsdp'), may hold values from 155.648 to 622.592
- norm_gains: float32 [2, 2048], P(None, 'fsdp'), may hold values from 0.5 to 1.5
- gains_first: float32 [2, 2048], P(None, 'fsdp'), may hold values from -80 to 80
- gains_second: float32 [2, 2048], P(None, 'fsdp'), may hold values from 409.6 to 3276.8
- conv_taps: float32 [3, 2048], P(None, 'fsdp'), may hold values from -2.4 to 2.4
- taps_first: float32 [3, 2048], P(None, 'fsdp'), may hold values from -80 to 80
- taps_second: float32 [3, 2048], P(None, 'fsdp'), may hold values from 729.088 to 2916.352
Outputs:
- block_output: bfloat16 [8192, 2048], P('fsdp')
- input_grad: float32 [8192, 2048], P('fsdp')
- inward_momentum: float32 [2048, 6144], P('fsdp')
- inward_variance: float32 [2048, 6144], P('fsdp')
- inward_updated: float32 [2048, 6144], P('fsdp')
- outward_momentum: float32 [2048, 2048], P('fsdp')
- outward_variance: float32 [2048, 2048], P('fsdp')
- outward_updated: float32 [2048, 2048], P('fsdp')
- gate_momentum: float32 [2048, 8192], P('fsdp')
- gate_variance: float32 [2048, 8192], P('fsdp')
- gate_updated: float32 [2048, 8192], P('fsdp')
- up_momentum: float32 [2048, 8192], P('fsdp')
- up_variance: float32 [2048, 8192], P('fsdp')
- up_updated: float32 [2048, 8192], P('fsdp')
- down_momentum: float32 [8192, 2048], P('fsdp')
- down_variance: float32 [8192, 2048], P('fsdp')
- down_updated: float32 [8192, 2048], P('fsdp')
- gains_momentum: float32 [2, 2048], P(None, 'fsdp')
- gains_variance: float32 [2, 2048], P(None, 'fsdp')
- gains_updated: float32 [2, 2048], P(None, 'fsdp')
- taps_momentum: float32 [3, 2048], P(None, 'fsdp')
- taps_variance: float32 [3, 2048], P(None, 'fsdp')
- taps_updated: float32 [3, 2048], P(None, 'fsdp')
The draws below stay inside these ranges and needn't reach their ends.
All inputs are finite; a program needn't handle non-finite values.
Results may differ from the reference program's by a relative error of at most 0.012.
The reference program's roundings to bfloat16 on the way count: a program that leaves them out, or rounds other values in their place, can miss the bound.
Values may be sent and summed in bfloat16 or wider, within the bound.
No kernel may reach another device: no remote copies, remote signals or barrier semaphores. Data moves between devices by JAX's collectives and lax.ppermute only.
A program may use at most 576 MiB of HBM per device.

```python
import math
import jax
import jax.numpy as jnp
from jax import lax

D = 2048
FF = 8192
STEP = 10
TOKENS = 8192
SEQ = 8192


def steps_of(own_key, extent, split, low, largest):
    level, own = 1.0, jax.random.fold_in(own_key, 6)
    for dim, blocks in split:
        steps = jnp.exp(jax.random.uniform(jax.random.fold_in(own, dim), (blocks,), jnp.float32, low / len(split), largest / len(split)))
        level = level * jnp.repeat(steps, extent[dim] // blocks).reshape([-1 if axis == dim else 1 for axis in range(len(extent))])
    return level


def noise(stream_key, extent, spread, most, split=(), held_as=jnp.bfloat16):
    factor_of = steps_of(stream_key, extent, split, -0.22, 0.18) if split else 1.0
    drawn = jax.random.normal(stream_key, extent, jnp.float32) * spread * factor_of
    return jnp.minimum(jnp.maximum(drawn, -most), most).astype(held_as)


def setup_inputs(seed: int = 0) -> dict:
    keys = jax.random.split(jax.random.key(seed), 24)
    return {
        "block_input": noise(keys[0], (TOKENS, D), 1.0, 6.0, ((0, 32),)),
        "cotangent": noise(keys[1], (TOKENS, D), 1.0, 6.0, ((0, 32),)),
        "inward_weight": noise(keys[2], (D, 3 * D), D ** -0.5, 0.125, ((0, 32),), jnp.float32),
        "inward_first": noise(keys[3], (D, 3 * D), (0.144 * TOKENS ** 0.5), 80.0, ((0, 32),), jnp.float32),
        "inward_second": jnp.clip(jnp.exp(math.log(2916.352) - 1.3862944 * jax.random.uniform(keys[4], (D, 3 * D), jnp.float32) ** steps_of(keys[4], (D, 3 * D), ((0, 32),), -0.2, 0.2)), 729.088, 2916.352),
        "outward_weight": noise(keys[5], (D, D), D ** -0.5, 0.125, ((0, 32),), jnp.float32),
        "outward_first": noise(keys[6], (D, D), (0.144 * TOKENS ** 0.5), 80.0, ((0, 32),), jnp.float32),
        "outward_second": jnp.clip(jnp.exp(math.log(2916.352) - 1.3862944 * jax.random.uniform(keys[7], (D, D), jnp.float32) ** steps_of(keys[7], (D, D), ((0, 32),), -0.2, 0.2)), 729.088, 2916.352),
        "gate_weight": noise(keys[8], (D, FF), D ** -0.5, 0.125, ((0, 32),), jnp.float32),
        "gate_first": noise(keys[9], (D, FF), (0.033 * TOKENS ** 0.5), 16.0, ((0, 32),), jnp.float32),
        "gate_second": jnp.clip(jnp.exp(math.log(155.648) - 1.3968765 * jax.random.uniform(keys[10], (D, FF), jnp.float32) ** steps_of(keys[10], (D, FF), ((0, 32),), -0.2, 0.2)), 38.5024, 155.648),
        "up_weight": noise(keys[11], (D, FF), D ** -0.5, 0.125, ((0, 32),), jnp.float32),
        "up_first": noise(keys[12], (D, FF), (0.033 * TOKENS ** 0.5), 16.0, ((0, 32),), jnp.float32),
        "up_second": jnp.clip(jnp.exp(math.log(155.648) - 1.3968765 * jax.random.uniform(keys[13], (D, FF), jnp.float32) ** steps_of(keys[13], (D, FF), ((0, 32),), -0.2, 0.2)), 38.5024, 155.648),
        "down_weight": noise(keys[14], (FF, D), FF ** -0.5, 0.0625, ((0, 32),), jnp.float32),
        "down_first": noise(keys[15], (FF, D), (0.067 * TOKENS ** 0.5), 32.0, ((0, 32),), jnp.float32),
        "down_second": jnp.clip(jnp.exp(math.log(622.592) - 1.3862944 * jax.random.uniform(keys[16], (FF, D), jnp.float32) ** steps_of(keys[16], (FF, D), ((0, 32),), -0.2, 0.2)), 155.648, 622.592),
        "norm_gains": jnp.clip(1.0 + 0.1 * jax.random.normal(keys[17], (2, D), jnp.float32), 0.5, 1.5),
        "gains_first": noise(keys[18], (2, D), (0.144 * TOKENS ** 0.5), 80.0, ((1, 32),), jnp.float32),
        "gains_second": jnp.clip(jnp.exp(math.log(3276.8) - 2.0794415 * jax.random.uniform(keys[19], (2, D), jnp.float32) ** steps_of(keys[19], (2, D), ((1, 32),), -0.2, 0.2)), 409.6, 3276.8),
        "conv_taps": noise(keys[20], (3, D), 0.6, 2.4, ((1, 32),), jnp.float32),
        "taps_first": noise(keys[21], (3, D), (0.144 * TOKENS ** 0.5), 80.0, ((1, 32),), jnp.float32),
        "taps_second": jnp.clip(jnp.exp(math.log(2916.352) - 1.3862944 * jax.random.uniform(keys[22], (3, D), jnp.float32) ** steps_of(keys[22], (3, D), ((1, 32),), -0.2, 0.2)), 729.088, 2916.352),
    }


EPS_NORM = 1e-05
BETA_ONE = 0.9
BETA_TWO = 0.95
ADAM_EPS = 1e-08
DECAY_RATE = 0.1
RATE_MATRIX = 0.01
RATE_VECTOR = 0.3

@jax.custom_vjp
def low(v):
    return lax.optimization_barrier(v.astype(jnp.bfloat16)).astype(jnp.float32)

@jax.custom_vjp
def low_back(v):
    return v

def low_keep(v):
    return (low(v), None)

def low_pass(kept, grad):
    return (grad,)

def back_keep(v):
    return (v, None)

def back_low(kept, grad):
    return (low(grad),)
low.defvjp(low_keep, low_pass)
low_back.defvjp(back_keep, back_low)

def product(operand, partner):
    return jnp.dot(operand, partner, precision=lax.Precision.HIGHEST, preferred_element_type=jnp.float32)

def rms_scale(values, gain):
    return values * lax.rsqrt(lax.optimization_barrier(jnp.mean(values * values, axis=-1, keepdims=True)) + EPS_NORM) * gain

def forward(inputs, inward_weight, outward_weight, gate_weight, up_weight, down_weight, norm_gains, conv_taps):
    gains_low = low(norm_gains)
    taps_low = low(conv_taps)
    flat = inputs.reshape(-1, D)
    normed = low(rms_scale(flat, gains_low[0]))
    mixed = low_back(product(normed, low(inward_weight)))
    b_part = mixed[:, :D]
    c_part = mixed[:, D:2 * D]
    x_part = mixed[:, 2 * D:]
    gated = (b_part * x_part).reshape(-1, SEQ, D)
    padded = jnp.pad(gated, ((0, 0), (2, 0), (0, 0)))
    convolved = taps_low[0] * padded[:, :SEQ] + taps_low[1] * padded[:, 1:SEQ + 1] + taps_low[2] * padded[:, 2:]
    branch_in = low(c_part * convolved.reshape(-1, D))
    branch = low_back(product(branch_in, low(outward_weight)))
    middle = flat + branch
    normed_two = low(rms_scale(middle, gains_low[1]))
    gate_value = low_back(product(normed_two, low(gate_weight)))
    up_value = low_back(product(normed_two, low(up_weight)))
    hidden = low(jax.nn.silu(gate_value) * up_value)
    result = middle + product(hidden, low(down_weight))
    return result.reshape(inputs.shape)

def adamw(weight, first, second, grad, rate, decay):
    first_new = BETA_ONE * first + (1.0 - BETA_ONE) * grad
    second_new = BETA_TWO * second + (1.0 - BETA_TWO) * grad * grad
    fix_one = 1.0 - BETA_ONE ** STEP
    fix_two = 1.0 - BETA_TWO ** STEP
    stepped = first_new / fix_one / (jnp.sqrt(second_new / fix_two) + ADAM_EPS)
    return (first_new, second_new, weight - rate * (stepped + decay * weight))

def reference(block_input, cotangent, inward_weight, inward_first, inward_second, outward_weight, outward_first, outward_second, gate_weight, gate_first, gate_second, up_weight, up_first, up_second, down_weight, down_first, down_second, norm_gains, gains_first, gains_second, conv_taps, taps_first, taps_second):
    seq_total = TOKENS // SEQ
    per_group = 1
    for candidate in range(1, seq_total + 1):
        if seq_total % candidate == 0 and candidate * SEQ <= 4096:
            per_group = candidate
    groups = seq_total // per_group
    inputs = block_input.astype(jnp.float32).reshape(groups, per_group, SEQ, D)
    cots = cotangent.astype(jnp.float32).reshape(groups, per_group, SEQ, D)
    params = (inward_weight, outward_weight, gate_weight, up_weight, down_weight, norm_gains, conv_taps)

    def step_group(carry, pair):
        group_in, group_cot = pair
        outputs, pullback = jax.vjp(forward, group_in, *params)
        grads = pullback(group_cot)
        new_carry = tuple((total + grad for total, grad in zip(carry, grads[1:])))
        return (new_carry, (outputs.astype(jnp.bfloat16), grads[0]))
    zeros = tuple((jnp.zeros(param.shape, jnp.float32) for param in params))
    totals, (outputs, in_grads) = lax.scan(step_group, zeros, (inputs, cots))
    block_output = outputs.reshape(TOKENS, D)
    input_grad = in_grads.reshape(TOKENS, D)
    inward_new = adamw(inward_weight, inward_first, inward_second, totals[0], RATE_MATRIX, DECAY_RATE)
    outward_new = adamw(outward_weight, outward_first, outward_second, totals[1], RATE_MATRIX, DECAY_RATE)
    gate_new = adamw(gate_weight, gate_first, gate_second, totals[2], RATE_MATRIX, DECAY_RATE)
    up_new = adamw(up_weight, up_first, up_second, totals[3], RATE_MATRIX, DECAY_RATE)
    down_new = adamw(down_weight, down_first, down_second, totals[4], RATE_MATRIX, DECAY_RATE)
    gains_new = adamw(norm_gains, gains_first, gains_second, totals[5], RATE_VECTOR, 0.0)
    taps_new = adamw(conv_taps, taps_first, taps_second, totals[6], RATE_VECTOR, 0.0)
    return (block_output, input_grad, inward_new[0], inward_new[1], inward_new[2], outward_new[0], outward_new[1], outward_new[2], gate_new[0], gate_new[1], gate_new[2], up_new[0], up_new[1], up_new[2], down_new[0], down_new[1], down_new[2], gains_new[0], gains_new[1], gains_new[2], taps_new[0], taps_new[1], taps_new[2])
```

```python
import jax
import jax.numpy as jnp
from jax import lax
from jax.sharding import Mesh
from jax.sharding import PartitionSpec as P

SEQ_BASE = 8192
STEP = 10

EPS_NORM = 1e-05
BETA_ONE = 0.9
BETA_TWO = 0.95
ADAM_EPS = 1e-08
DECAY_RATE = 0.1
RATE_MATRIX = 0.01
RATE_VECTOR = 0.3

AXES = ("p", "y", "x", "c")
PLANE = ("y", "x", "c")
COLUMN = ("p", "c")
CROSS = ("y", "x")
LOW = jnp.bfloat16


def forward_dot(operand, partner):
    return jnp.dot(operand, partner, preferred_element_type=jnp.float32)


def over_tokens(operand, partner):
    return lax.dot_general(
        operand, partner, (((0,), (0,)), ((), ())), preferred_element_type=jnp.float32
    )


def against_rows(operand, partner):
    return lax.dot_general(
        operand, partner, (((1,), (1,)), ((), ())), preferred_element_type=jnp.float32
    )


def rms_parts(values):
    scale = lax.rsqrt(jnp.mean(values * values, axis=-1, keepdims=True) + EPS_NORM)
    return (scale, values * scale)


def norm_back(upstream, normal, scale, gain):
    scaled = upstream * gain
    return scale * (scaled - normal * jnp.mean(scaled * normal, axis=-1, keepdims=True))


def adamw(weight, first, second, grad, rate, decay):
    first_new = BETA_ONE * first + (1.0 - BETA_ONE) * grad
    second_new = BETA_TWO * second + (1.0 - BETA_TWO) * grad * grad
    fix_one = 1.0 - BETA_ONE**STEP
    fix_two = 1.0 - BETA_TWO**STEP
    stepped = first_new / fix_one / (jnp.sqrt(second_new / fix_two) + ADAM_EPS)
    return (first_new, second_new, weight - rate * (stepped + decay * weight))


def gather(block, axes):
    return lax.all_gather(block, axes, axis=0, tiled=True)


def scatter(term, axes):
    return lax.psum_scatter(term, axes, scatter_dimension=0, tiled=True)


def exchange(blocks, axes):
    return lax.all_to_all(blocks, axes, split_axis=0, concat_axis=0, tiled=True)


def along_planes(block, distance):
    count = lax.axis_size("p")
    route = [(i - distance, i) for i in range(count) if 0 <= i - distance < count]
    return lax.ppermute(block, "p", route)


def on_device(
    block_input,
    cotangent,
    inward_weight,
    inward_first,
    inward_second,
    outward_weight,
    outward_first,
    outward_second,
    gate_weight,
    gate_first,
    gate_second,
    up_weight,
    up_first,
    up_second,
    down_weight,
    down_first,
    down_second,
    norm_gains,
    gains_first,
    gains_second,
    conv_taps,
    taps_first,
    taps_second,
):
    planes = lax.axis_size("p")
    tok_rows, d = block_input.shape
    d_rows = inward_weight.shape[0]
    ff = gate_weight.shape[1]
    ff_rows = down_weight.shape[0]
    plane_rows = 8 * tok_rows
    seq_len = min(SEQ_BASE, plane_rows * planes)
    feats = d // 8
    plane = lax.axis_index("p")
    place = lax.axis_index(PLANE)

    small_local = jnp.concatenate([norm_gains, conv_taps], axis=0).T.astype(LOW)
    small_full = gather(small_local, AXES).astype(jnp.float32)
    gain_one = small_full[:, 0]
    gain_two = small_full[:, 1]
    taps_here = lax.dynamic_index_in_dim(
        small_full.reshape(planes, 8, d_rows, 5), place, axis=1, keepdims=False
    ).reshape(feats, 5)
    tap_zero = taps_here[:, 2]
    tap_one = taps_here[:, 3]
    tap_two = taps_here[:, 4]

    inward_low = inward_weight.astype(LOW)
    inward_sent = inward_low.reshape(d_rows, 3, planes, 8, d_rows).transpose(3, 0, 1, 2, 4)
    inward_part = gather(exchange(inward_sent.reshape(8, d_rows, 3 * feats), PLANE), "p")
    inward_part = inward_part.reshape(d, 3 * feats)
    outward_full = gather(gather(outward_weight.astype(LOW), "p"), PLANE)

    gate_low = gate_weight.astype(LOW)
    up_low = up_weight.astype(LOW)

    def ffn_part(low):
        sent = low.reshape(d_rows, planes, 4, 2, ff_rows).transpose(1, 3, 0, 2, 4)
        got = exchange(sent.reshape(2 * planes, d_rows, 4 * ff_rows), COLUMN)
        whole = gather(got[None], CROSS)
        whole = whole.reshape(4, planes, 2, d_rows, 4 * ff_rows).transpose(1, 0, 2, 3, 4)
        return whole.reshape(d, 4 * ff_rows)

    gate_part = ffn_part(gate_low)
    up_part = ffn_part(up_low)
    down_part = gather(down_weight.astype(LOW), CROSS)

    inputs = block_input.astype(jnp.float32)
    scale_one, normal_one = rms_parts(inputs)
    normed_one = gather((normal_one * gain_one).astype(LOW), PLANE)
    mixed = forward_dot(normed_one, inward_part)
    b_part = mixed[:, :feats]
    c_part = mixed[:, feats : 2 * feats]
    x_part = mixed[:, 2 * feats :]
    gated = b_part * x_part
    starts_here = plane * plane_rows % seq_len == 0
    previous = jnp.where(starts_here, 0.0, along_planes(gated[plane_rows - 2 :], 1))
    extended = jnp.concatenate([previous, gated], axis=0)
    convolved = (
        tap_zero * extended[:plane_rows]
        + tap_one * extended[1 : plane_rows + 1]
        + tap_two * extended[2:]
    )
    branch_feats = (c_part * convolved).astype(LOW)
    branch_in = exchange(branch_feats.reshape(8, tok_rows, feats), PLANE)
    branch_in = branch_in.transpose(1, 0, 2).reshape(tok_rows, d)
    middle = inputs + forward_dot(branch_in, outward_full)
    scale_two, normal_two = rms_parts(middle)

    normed_two = gather((normal_two * gain_two).astype(LOW), COLUMN)
    upstream = gather(cotangent, COLUMN)
    gate_value = forward_dot(normed_two, gate_part)
    up_value = forward_dot(normed_two, up_part)
    sigmoid_gate = jax.nn.sigmoid(gate_value)
    silu_gate = gate_value * sigmoid_gate
    hidden = (silu_gate * up_value).astype(LOW)
    hidden_grad = against_rows(upstream, down_part)
    gate_grad = (
        hidden_grad * up_value * sigmoid_gate * (1.0 + gate_value * (1.0 - sigmoid_gate))
    ).astype(LOW)
    up_grad = (hidden_grad * silu_gate).astype(LOW)
    normed_two_grad = against_rows(gate_grad, gate_part) + against_rows(up_grad, up_part)
    normed_two_grad = scatter(normed_two_grad.astype(LOW), COLUMN).astype(jnp.float32)
    result = scatter(forward_dot(hidden, down_part).astype(LOW), COLUMN)
    block_output = (middle + result.astype(jnp.float32)).astype(LOW)

    down_sum = scatter(over_tokens(hidden, upstream).astype(LOW), CROSS).astype(jnp.float32)

    def ffn_sum(grad):
        term = over_tokens(normed_two, grad).astype(LOW)
        term = term.reshape(planes, 4, 2, d_rows, 4 * ff_rows).transpose(1, 0, 2, 3, 4)
        own = scatter(term, CROSS).reshape(2 * planes, d_rows, 4 * ff_rows)
        own = exchange(own, COLUMN).reshape(planes, 2, d_rows, 4, ff_rows)
        return own.transpose(2, 0, 3, 1, 4).reshape(d_rows, ff).astype(jnp.float32)

    gate_sum = ffn_sum(gate_grad)
    up_sum = ffn_sum(up_grad)

    middle_grad = cotangent.astype(jnp.float32) + norm_back(
        normed_two_grad, normal_two, scale_two, gain_two
    )
    branch_grad = middle_grad.astype(LOW)
    outward_sum = scatter(
        scatter(over_tokens(branch_in, branch_grad).astype(LOW), PLANE), "p"
    ).astype(jnp.float32)
    branch_in_grad = against_rows(branch_grad, outward_full).astype(LOW)
    branch_in_grad = branch_in_grad.reshape(tok_rows, 8, feats).transpose(1, 0, 2)
    branch_in_grad = exchange(branch_in_grad, PLANE).reshape(plane_rows, feats)
    branch_in_grad = branch_in_grad.astype(jnp.float32)
    c_grad = branch_in_grad * convolved
    conv_grad = branch_in_grad * c_part
    ext_grad = (
        jnp.pad(tap_zero * conv_grad, ((0, 2), (0, 0)))
        + jnp.pad(tap_one * conv_grad, ((1, 1), (0, 0)))
        + jnp.pad(tap_two * conv_grad, ((2, 0), (0, 0)))
    )
    tap_grads = jnp.stack(
        [
            jnp.sum(conv_grad * extended[offset : offset + plane_rows], axis=0)
            for offset in range(3)
        ],
        axis=1,
    )
    returned = along_planes(jnp.where(starts_here, 0.0, ext_grad[:2]), -1)
    gated_grad = ext_grad[2:] + jnp.pad(returned, ((plane_rows - 2, 0), (0, 0)))
    mixed_grad = jnp.concatenate([gated_grad * x_part, c_grad, gated_grad * b_part], axis=1)
    mixed_grad = mixed_grad.astype(LOW)
    normed_one_grad = against_rows(mixed_grad, inward_part)
    normed_one_grad = scatter(normed_one_grad.astype(LOW), PLANE).astype(jnp.float32)
    input_grad = middle_grad + norm_back(normed_one_grad, normal_one, scale_one, gain_one)

    inward_term = over_tokens(normed_one, mixed_grad).astype(LOW)
    inward_own = scatter(inward_term, "p").reshape(8, d_rows, 3 * feats)
    inward_own = exchange(inward_own, PLANE).reshape(8, d_rows, 3, planes, d_rows)
    inward_sum = inward_own.transpose(1, 2, 3, 0, 4).reshape(d_rows, 3 * d).astype(jnp.float32)

    own_gains = norm_gains.astype(LOW).astype(jnp.float32)
    gain_one_grad = jnp.sum(inward_low.astype(jnp.float32) * inward_sum, axis=1) / own_gains[0]
    gain_two_grad = (
        jnp.sum(gate_low.astype(jnp.float32) * gate_sum, axis=1)
        + jnp.sum(up_low.astype(jnp.float32) * up_sum, axis=1)
    ) / own_gains[1]
    gains_grad = jnp.stack([gain_one_grad, gain_two_grad])
    taps_grad = scatter(tap_grads, "p").T

    inward_new = adamw(
        inward_weight, inward_first, inward_second, inward_sum, RATE_MATRIX, DECAY_RATE
    )
    outward_new = adamw(
        outward_weight, outward_first, outward_second, outward_sum, RATE_MATRIX, DECAY_RATE
    )
    gate_new = adamw(gate_weight, gate_first, gate_second, gate_sum, RATE_MATRIX, DECAY_RATE)
    up_new = adamw(up_weight, up_first, up_second, up_sum, RATE_MATRIX, DECAY_RATE)
    down_new = adamw(down_weight, down_first, down_second, down_sum, RATE_MATRIX, DECAY_RATE)
    gains_new = adamw(norm_gains, gains_first, gains_second, gains_grad, RATE_VECTOR, 0.0)
    taps_new = adamw(conv_taps, taps_first, taps_second, taps_grad, RATE_VECTOR, 0.0)
    return (
        block_output,
        input_grad,
        *inward_new,
        *outward_new,
        *gate_new,
        *up_new,
        *down_new,
        *gains_new,
        *taps_new,
    )


def solution(mesh):
    devices = mesh.devices.reshape(-1, 2, 2, 2)
    rows = P(AXES, None)
    columns = P(None, AXES)
    return jax.shard_map(
        on_device,
        mesh=Mesh(devices, AXES),
        in_specs=(rows,) * 17 + (columns,) * 6,
        out_specs=(rows,) * 17 + (columns,) * 6,
        check_vma=False,
    )
```

```python
import functools

import jax
import jax.numpy as jnp
from jax import lax
from jax.experimental import pallas as pl
from jax.experimental.pallas import tpu as pltpu
from jax.sharding import Mesh
from jax.sharding import PartitionSpec as P

SEQ_BASE = 8192
STEP = 10

EPS_NORM = 1e-05
BETA_ONE = 0.9
BETA_TWO = 0.95
ADAM_EPS = 1e-08
DECAY_RATE = 0.1
RATE_MATRIX = 0.01
RATE_VECTOR = 0.3

AXES = ("h", "l", "y", "x", "c")
GROUP = ("l", "x", "c")
CLASS = ("h", "y")
LOW = jnp.bfloat16
F32 = jnp.float32


def forward_dot(operand, partner):
    return jnp.dot(operand, partner, preferred_element_type=jnp.float32)


def over_tokens(operand, partner):
    return lax.dot_general(
        operand, partner, (((0,), (0,)), ((), ())), preferred_element_type=jnp.float32
    )


def against_rows(operand, partner):
    return lax.dot_general(
        operand, partner, (((1,), (1,)), ((), ())), preferred_element_type=jnp.float32
    )


def rms_parts(values):
    scale = lax.rsqrt(jnp.mean(values * values, axis=-1, keepdims=True) + EPS_NORM)
    return (scale, values * scale)


def norm_back(upstream, normal, scale, gain):
    scaled = upstream * gain
    return scale * (scaled - normal * jnp.mean(scaled * normal, axis=-1, keepdims=True))


def adamw(weight, first, second, grad, rate, decay):
    first_new = BETA_ONE * first + (1.0 - BETA_ONE) * grad
    second_new = BETA_TWO * second + (1.0 - BETA_TWO) * grad * grad
    fix_one = 1.0 - BETA_ONE**STEP
    fix_two = 1.0 - BETA_TWO**STEP
    stepped = first_new / fix_one / (jnp.sqrt(second_new / fix_two) + ADAM_EPS)
    return (first_new, second_new, weight - rate * (stepped + decay * weight))


def after(value, *others):
    return lax.optimization_barrier((value, *others))[0]


def together(*values):
    return lax.optimization_barrier(values)


def swap(block, axis):
    return lax.ppermute(block, axis, [(0, 1), (1, 0)])


def turn(block, distance):
    count = lax.axis_size("h")
    return lax.ppermute(block, "h", [((i + distance) % count, i) for i in range(count)])


def in_order(pieces, axis):
    own, other = pieces
    first = lax.axis_index(axis) == 0
    return jnp.stack([jnp.where(first, own, other), jnp.where(first, other, own)])


def class_small(block):
    if lax.axis_size("h") == 2:
        block = in_order((block, turn(block, 1)), "h")
    else:
        block = lax.all_gather(block, "h", axis=0, tiled=False)
    return in_order((block, swap(block, "y")), "y")


def group_small(block):
    for axis in ("l", "x", "c"):
        block = in_order((block, swap(block, axis)), axis)
    return block.transpose(4, 2, 3, 1, 0, 5, 6)


def turns(block):
    return [turn(block, i) for i in range(1, lax.axis_size("h"))]


def swaps(blocks):
    return [swap(block, "y") for block in blocks]


def class_stack(own, by_h, by_y, by_both):
    count = lax.axis_size("h")
    rows = []
    for first, rest in ((own, by_h), (by_y, by_both)):
        rows += first
        for i in range(count - 1):
            rows += [part[i] for part in rest]
    return jnp.concatenate(rows, axis=0)


def class_lend(term):
    half = term.shape[0] // 2
    return term[:half] + swap(term[half:], "y")


def class_settle(column):
    count = lax.axis_size("h")
    rows = column.shape[0] // count
    total = column[:rows].astype(F32)
    for i in range(1, count):
        total = total + turn(column[i * rows : (i + 1) * rows], -i).astype(F32)
    return total.astype(LOW)


def class_scatter(term):
    return class_settle(class_lend(term))


def group_gather(block):
    return lax.all_gather(block, GROUP, axis=0, tiled=True)


def group_exchange(blocks):
    return lax.all_to_all(blocks, GROUP, split_axis=0, concat_axis=0, tiled=True)


def core_rows(array, own):
    core = lax.axis_index("c") if own else 1 - lax.axis_index("c")
    rows = array.shape[0] // 8
    return jnp.concatenate(
        [lax.dynamic_slice_in_dim(array, (2 * i + core) * rows, rows, axis=0) for i in range(4)],
        axis=0,
    )


def group_lend(near, far):
    quarter = near.shape[0] // 4
    half = quarter // 2
    got = swap(far, "c")
    mine_l, mine_x = lax.axis_index("l"), lax.axis_index("x")

    def block(dl, dx):
        place = (mine_l ^ dl) * 2 + (mine_x ^ dx)
        return tuple(
            lax.dynamic_slice_in_dim(part, place * quarter, quarter, axis=0) for part in (near, got)
        )

    corner = sum(block(1, 1))
    from_l = swap(corner[:half], "l")
    from_x = swap(corner[half:], "x")
    return from_l, from_x, block


def group_settle(from_l, from_x, block):
    near_x, got_x = block(0, 1)
    near_l, got_l = block(1, 0)
    by_x = near_x + got_x + jnp.concatenate([from_l, jnp.zeros_like(from_l)], axis=0)
    by_l = near_l + got_l + jnp.concatenate([jnp.zeros_like(from_x), from_x], axis=0)
    own = sum(block(0, 0))
    return own, swap(by_x, "x"), swap(by_l, "l")


def rearranged(values, to_class):
    count = lax.axis_size("h")
    rest = values.shape[-1] // (4 * count)
    blocks = [values[..., i * rest : (i + 1) * rest] for i in range(4 * count)]
    mine_h, mine_y = lax.axis_index("h"), lax.axis_index("y")
    if to_class:
        lists = [
            [[blocks[((h * 2) + l) * 2 + y] for h in range(count)] for y in range(2)] for l in range(2)
        ]
    else:
        lists = [
            [[blocks[(y * count + h) * 2 + l] for h in range(count)] for y in range(2)] for l in range(2)
        ]

    def pick(l, y, h):
        chosen = None
        for shift in range(count):
            at = (h + shift) % count if to_class else (h - shift) % count
            here = jnp.where(mine_y == 0, lists[l][y][at], lists[l][1 - y][at])
            chosen = here if chosen is None else jnp.where(mine_h == shift, here, chosen)
        return chosen

    if to_class:
        order = [(l, y, h) for y in range(2) for h in range(count) for l in range(2)]
    else:
        order = [(l, y, h) for h in range(count) for l in range(2) for y in range(2)]
    return jnp.concatenate([pick(*place) for place in order], axis=-1)


def class_rows(array):
    count = lax.axis_size("h")
    split = array.reshape(2, count, -1, array.shape[1])
    mine_h, mine_y = lax.axis_index("h"), lax.axis_index("y")
    pieces = []
    for h in range(count):
        for y in range(2):
            at = [mine_y ^ y, (h - mine_h) & (count - 1), 0, 0]
            pieces.append(lax.dynamic_slice(split, at, (1, 1, *split.shape[2:]))[0, 0])
    return jnp.concatenate(pieces, axis=0)


def class_pieces(array):
    count = lax.axis_size("h")
    split = array.reshape(count, 2, -1, array.shape[1])
    mine_h, mine_y = lax.axis_index("h"), lax.axis_index("y")
    pieces = []
    for dy in range(2):
        for dh in range(count):
            at = [(mine_h + dh) & (count - 1), mine_y ^ dy, 0, 0]
            pieces.append(lax.dynamic_slice(split, at, (1, 1, *split.shape[2:]))[0, 0])
    return jnp.concatenate(pieces, axis=0)


def places(count):
    return [(h, l, y, x, c) for h in range(count) for l in (0, 1) for y in (0, 1) for x in (0, 1) for c in (0, 1)]


def pack_body(count, inward_ref, gate_ref, up_ref, inward_out, ffn_out):
    d_rows = inward_ref.shape[1] // (48 * count)
    ff_rows = gate_ref.shape[1] // (16 * count)
    feats, units = 2 * count * d_rows, 2 * count * ff_rows
    for at, (h, l, y, x, c) in enumerate(places(count)):
        to, slot = (l * 2 + x) * 2 + c, h * 2 + y
        for kind, ref in enumerate((gate_ref, up_ref)):
            block = ref[:, at * ff_rows : (at + 1) * ff_rows].astype(LOW)
            ffn_out[to, :, kind * units + slot * ff_rows : kind * units + (slot + 1) * ff_rows] = block
    for part in range(3):
        for to in range(8):
            l, x, c = to // 4, to // 2 % 2, to % 2
            blocks = []
            for h in range(count):
                for y in range(2):
                    at = part * 16 * count + (((h * 2 + l) * 2 + y) * 2 + x) * 2 + c
                    blocks.append(inward_ref[:, at * d_rows : (at + 1) * d_rows])
            block = jnp.concatenate(blocks, axis=1).astype(LOW)
            inward_out[to, :, part * feats : (part + 1) * feats] = block


def packed(inward, gate, up, count):
    d_rows, ff = gate.shape
    feats, units = inward.shape[1] // 24, ff // 8
    if d_rows % 64 or units % (256 * count):
        sent = inward.astype(LOW).reshape(d_rows, 3, count, 2, 2, 2, 2, -1)
        sent = sent.transpose(3, 5, 6, 0, 1, 2, 4, 7).reshape(8, d_rows, 3 * feats)
        both = jnp.stack([gate.astype(LOW), up.astype(LOW)], axis=1)
        both = both.reshape(d_rows, 2, count, 2, 2, 2, 2, -1).transpose(3, 5, 6, 0, 1, 2, 4, 7)
        return sent, both.reshape(8, d_rows, 2 * units)
    rows = 16
    return pl.pallas_call(
        functools.partial(pack_body, count),
        grid=(d_rows // rows,),
        in_specs=[
            pl.BlockSpec((rows, 24 * feats), lambda i: (i, 0)),
            pl.BlockSpec((rows, ff), lambda i: (i, 0)),
            pl.BlockSpec((rows, ff), lambda i: (i, 0)),
        ],
        out_specs=[
            pl.BlockSpec((8, rows, 3 * feats), lambda i: (0, i, 0)),
            pl.BlockSpec((8, rows, 2 * units), lambda i: (0, i, 0)),
        ],
        out_shape=[
            jax.ShapeDtypeStruct((8, d_rows, 3 * feats), LOW),
            jax.ShapeDtypeStruct((8, d_rows, 2 * units), LOW),
        ],
        compiler_params=pltpu.CompilerParams(vmem_limit_bytes=32 * 2**20),
        cost_estimate=pl.CostEstimate(flops=0, transcendentals=0, bytes_accessed=6 * d_rows * (24 * feats + 2 * ff)),
    )(inward, gate, up)


def update_body(pieces, got_ref, weight_ref, first_ref, second_ref, first_out, second_out, weight_out, dot_out):
    width = weight_ref.shape[1] // len(pieces)

    @pl.when(pl.program_id(0) == 0)
    def _():
        dot_out[...] = jnp.zeros_like(dot_out)

    total = jnp.zeros((weight_ref.shape[0], 128), F32)
    for group in range(0, len(pieces), max(1, 128 // width)):
        parts = pieces[group : group + max(1, 128 // width)]
        grad = [got_ref[tuple(at)][:, lane : lane + width].astype(F32) for *at, lane in parts]
        grad = jnp.concatenate(grad, axis=1) if len(grad) > 1 else grad[0]
        here = slice(group * width, group * width + grad.shape[1])
        weight = weight_ref[:, here]
        first, second, updated = adamw(
            weight, first_ref[:, here], second_ref[:, here], grad, RATE_MATRIX, DECAY_RATE
        )
        first_out[:, here] = first
        second_out[:, here] = second
        weight_out[:, here] = updated
        dots = weight.astype(LOW).astype(F32) * grad
        for lane in range(0, grad.shape[1], 128):
            total += dots[:, lane : lane + 128]
    dot_out[...] += total


def updated_columns(got, weight, first, second, count, parts):
    rows, columns = weight.shape
    width = columns // (16 * count * parts)
    if width % (128 if parts == 1 else 64) or rows % 16:
        grad = got.reshape(2, 2, 2, rows, parts, count, 2, width).transpose(3, 4, 5, 0, 6, 1, 2, 7)
        grad = grad.reshape(rows, columns).astype(F32)
        new = adamw(weight, first, second, grad, RATE_MATRIX, DECAY_RATE)
        return new, jnp.sum(weight.astype(LOW).astype(F32) * grad, axis=1)
    if parts == 1:
        grid = (4 * count,)
        got = got.reshape(2, 4, rows, 2 * count * width)
        got_spec = pl.BlockSpec((1, 4, rows, width), lambda k: (k // 2 % 2, 0, 0, k // 4 * 2 + k % 2))
        pieces = [(0, q, 0) for q in range(4)]
        block = 4 * width
    else:
        grid = (parts,)
        got_spec = pl.BlockSpec((8, rows, 2 * count * width), lambda k: (0, 0, k))
        pieces = [((l * 2 + x) * 2 + c, (h * 2 + y) * width) for h, l, y, x, c in places(count)]
        block = 16 * count * width
    spec = pl.BlockSpec((rows, block), lambda k: (0, k))
    shape = jax.ShapeDtypeStruct(weight.shape, F32)
    *new, dots = pl.pallas_call(
        functools.partial(update_body, pieces),
        grid=grid,
        in_specs=[got_spec, spec, spec, spec],
        out_specs=[spec, spec, spec, pl.BlockSpec((rows, 128), lambda k: (0, 0))],
        out_shape=[shape, shape, shape, jax.ShapeDtypeStruct((rows, 128), F32)],
        compiler_params=pltpu.CompilerParams(vmem_limit_bytes=32 * 2**20),
        cost_estimate=pl.CostEstimate(
            flops=20 * rows * columns, transcendentals=2 * rows * columns, bytes_accessed=26 * rows * columns
        ),
    )(got, weight, first, second)
    return tuple(new), jnp.sum(dots, axis=1)


def step_h(block, distance):
    count = lax.axis_size("h")
    route = []
    for i in range(count):
        if 0 <= i - distance < count:
            y_to = 0 if distance == 1 else 1
            route.append((2 * (i - distance) + 1 - y_to, 2 * i + y_to))
    return lax.ppermute(block, CLASS, route)


def on_device(
    block_input,
    cotangent,
    inward_weight,
    inward_first,
    inward_second,
    outward_weight,
    outward_first,
    outward_second,
    gate_weight,
    gate_first,
    gate_second,
    up_weight,
    up_first,
    up_second,
    down_weight,
    down_first,
    down_second,
    norm_gains,
    gains_first,
    gains_second,
    conv_taps,
    taps_first,
    taps_second,
):
    count = lax.axis_size("h")
    tok_rows, d = block_input.shape
    d_rows = inward_weight.shape[0]
    ff = gate_weight.shape[1]
    ff_rows = down_weight.shape[0]
    group_rows = 8 * tok_rows
    near_rows = 4 * tok_rows
    seq_len = min(SEQ_BASE, group_rows * 2 * count)
    feats = d // 8
    units = ff // 8
    mine = {axis: lax.axis_index(axis) for axis in AXES}

    small = class_small(jnp.concatenate([norm_gains, conv_taps], axis=0).astype(LOW))
    outward_low, down_low, small = together(
        outward_weight.astype(LOW), down_weight.astype(LOW), small
    )
    outward_h, outward_y = turns(outward_low), swap(outward_low, "y")
    down_a, down_b = down_low[: ff_rows // 2], down_low[ff_rows // 2 :]
    down_ah, down_ay = turns(down_a), swap(down_a, "y")
    small = group_small(small)
    inward_sent, ffn_sent = packed(inward_weight, gate_weight, up_weight, count)
    inward_got = group_exchange(after(inward_sent, small)).reshape(8 * d_rows, 3 * feats)
    block_here = rearranged(block_input, True)
    inward_got, ffn_sent, outward_h, outward_y, down_ah, down_ay, down_b, small, block_here = together(
        inward_got, ffn_sent, outward_h, outward_y, down_ah, down_ay, down_b, small, block_here
    )

    inward_h, inward_y = turns(inward_got), swap(inward_got, "y")
    ffn_got = group_exchange(ffn_sent).reshape(8 * d_rows, 2 * units)
    inputs_low = group_gather(block_here)
    outward_hy, down_ahy = swaps(outward_h), swaps(down_ah)
    inward_h, inward_y, outward_hy, down_ahy, ffn_got = together(
        inward_h, inward_y, outward_hy, down_ahy, ffn_got
    )
    outward_part = class_stack([outward_low], [outward_h], [outward_y], [outward_hy])
    outward_full = group_gather(class_rows(outward_part))

    half_d = 4 * d_rows
    gate_a, gate_b = ffn_got[:half_d, :units], ffn_got[half_d:, :units]
    up_low = ffn_got[:, units:]
    inward_hy = swaps(inward_h)
    gate_ah, gate_ay = turns(gate_a), swap(gate_a, "y")
    inward_hy, gate_ah, gate_ay, gate_b, up_low, inputs_low = together(
        inward_hy, gate_ah, gate_ay, gate_b, up_low, inputs_low
    )
    inward_part = class_stack([inward_got], [inward_h], [inward_y], [inward_hy])
    gate_bh, gate_by, gate_ahy = turns(gate_b), swap(gate_b, "y"), swaps(gate_ah)
    small = small.astype(F32)

    gain_one = small[..., 0, :].reshape(d)
    gain_two = small[..., 1, :].reshape(d)
    taps_here = lax.dynamic_slice(
        small, (0, mine["l"], 0, mine["x"], mine["c"], 2, 0), (count, 1, 2, 1, 1, 3, d_rows)
    )
    taps_here = taps_here.reshape(2 * count, 3, d_rows).transpose(1, 0, 2).reshape(3, feats)
    tap_zero, tap_one, tap_two = taps_here[0], taps_here[1], taps_here[2]

    _, normed_one = rms_parts(inputs_low.astype(F32))
    normed_one = (normed_one * rearranged(gain_one, True)).astype(LOW)
    mixed = forward_dot(normed_one, inward_part).reshape(2, near_rows, 3 * feats)
    b_part = mixed[..., :feats]
    c_part = mixed[..., feats : 2 * feats]
    x_part = mixed[..., 2 * feats :]
    gated = b_part * x_part
    tails = gated[:, near_rows - 2 :]
    runs = (mine["h"] * 2 + jnp.arange(2)) * 2 + mine["y"]
    starts_here = (runs * near_rows % seq_len == 0).reshape(2, 1, 1)
    beside = swap(tails, "y")
    below = step_h(tails[1], 1)
    before = jnp.where(mine["y"] == 1, beside, jnp.stack([below, beside[0]]))
    before = jnp.where(starts_here, 0.0, before)
    extended = jnp.concatenate([before, gated], axis=1)
    convolved = (
        tap_zero * extended[:, :near_rows]
        + tap_one * extended[:, 1 : near_rows + 1]
        + tap_two * extended[:, 2:]
    )
    branch_feats = (c_part * convolved).astype(LOW).reshape(group_rows, feats)
    branch_feats, gate_bh, gate_by, gate_ahy, up_low = together(
        branch_feats, gate_bh, gate_by, gate_ahy, up_low
    )
    up_h, up_y, gate_bhy = turns(up_low), swap(up_low, "y"), swaps(gate_bh)
    branch_in = group_exchange(branch_feats.reshape(8, tok_rows, feats))
    branch_in = branch_in.transpose(1, 0, 2).reshape(tok_rows, d)
    inputs = block_input.astype(F32)
    middle = inputs + forward_dot(branch_in, outward_full)
    scale_two, normal_two = rms_parts(middle)

    normed_two = rearranged((normal_two * gain_two).astype(LOW), True)
    normed_two, up_h, up_y, gate_bhy, down_b = together(normed_two, up_h, up_y, gate_bhy, down_b)
    upstream = group_gather(after(cotangent, normed_two))
    normed_two = group_gather(normed_two)
    down_bh, down_by, up_hy = turns(down_b), swap(down_b, "y"), swaps(up_h)
    down_bh, down_by, up_hy = together(down_bh, down_by, up_hy)
    down_bhy = swaps(down_bh)
    gate_part = class_stack(
        [gate_a, gate_b], [gate_ah, gate_bh], [gate_ay, gate_by], [gate_ahy, gate_bhy]
    )
    up_part = class_stack([up_low], [up_h], [up_y], [up_hy])
    down_part = class_stack(
        [down_a, down_b], [down_ah, down_bh], [down_ay, down_by], [down_ahy, down_bhy]
    )
    down_part = class_rows(down_part)
    gate_value = forward_dot(normed_two, gate_part)
    up_value = forward_dot(normed_two, up_part)
    sigmoid_gate = jax.nn.sigmoid(gate_value)
    silu_gate = gate_value * sigmoid_gate
    hidden = (silu_gate * up_value).astype(LOW)
    result = forward_dot(hidden, down_part).astype(LOW)
    hidden, result = together(hidden, result)
    result = lax.psum_scatter(result, GROUP, scatter_dimension=0, tiled=True)
    down_term = class_pieces(over_tokens(hidden, upstream).astype(LOW))
    hidden, down_term = together(hidden, down_term)
    down_column = class_lend(down_term)
    hidden_grad = against_rows(upstream, down_part)
    gate_grad = hidden_grad * up_value * sigmoid_gate * (1.0 + gate_value * (1.0 - sigmoid_gate))
    up_grad = hidden_grad * silu_gate
    gate_grad = gate_grad.astype(LOW)
    up_grad = up_grad.astype(LOW)

    def ffn_back(own):
        part = against_rows(core_rows(gate_grad, own), gate_part)
        return (part + against_rows(core_rows(up_grad, own), up_part)).astype(LOW)

    far = ffn_back(False)
    far, down_column = together(far, down_column)
    down_sum = class_settle(down_column)
    near = ffn_back(True)
    gate_term = over_tokens(normed_two, gate_grad).astype(LOW)
    far, near, gate_term = together(far, near, gate_term)
    gate_column = class_lend(gate_term)
    up_term = over_tokens(normed_two, up_grad).astype(LOW)
    from_l, from_x, block = group_lend(near, far)
    from_l, from_x, gate_column, up_term, down_sum = together(
        from_l, from_x, gate_column, up_term, down_sum
    )
    down_sum = down_sum.astype(F32)
    gate_own = class_settle(gate_column)
    up_column = class_lend(up_term)
    *parts, gate_own, up_column, result = together(
        *group_settle(from_l, from_x, block), gate_own, up_column, result
    )
    block_output = (middle + result.astype(F32)).astype(LOW)
    normed_two_grad = rearranged(sum(part.astype(F32) for part in parts), False)

    middle_grad = cotangent.astype(F32) + norm_back(
        normed_two_grad, normal_two, scale_two, gain_two
    )
    branch_grad = middle_grad.astype(LOW)
    branch_in_grad = against_rows(branch_grad, outward_full).astype(LOW)
    branch_in_grad = group_exchange(branch_in_grad.reshape(tok_rows, 8, feats).transpose(1, 0, 2))
    branch_in_grad = branch_in_grad.reshape(2, near_rows, feats).astype(F32)
    branch_grad_full = group_gather(branch_grad)

    c_grad = branch_in_grad * convolved
    conv_grad = branch_in_grad * c_part
    ext_grad = (
        jnp.pad(tap_zero * conv_grad, ((0, 0), (0, 2), (0, 0)))
        + jnp.pad(tap_one * conv_grad, ((0, 0), (1, 1), (0, 0)))
        + jnp.pad(tap_two * conv_grad, ((0, 0), (2, 0), (0, 0)))
    )
    tap_grads = jnp.stack(
        [
            jnp.sum(conv_grad * extended[:, offset : offset + near_rows], axis=(0, 1))
            for offset in range(3)
        ],
        axis=1,
    )
    firsts = jnp.where(starts_here, 0.0, ext_grad[:, :2])
    beside = swap(firsts, "y")
    above = step_h(firsts[0], -1)
    returned = jnp.where(mine["y"] == 0, beside, jnp.stack([beside[1], above]))

    returned, gate_own, up_column = together(returned, gate_own, up_column)
    gate_own = group_exchange(gate_own.reshape(8, d_rows, units))
    up_own = class_settle(up_column)
    gated_grad = ext_grad[:, 2:] + jnp.pad(returned, ((0, 0), (near_rows - 2, 0), (0, 0)))
    mixed_grad = jnp.concatenate([gated_grad * x_part, c_grad, gated_grad * b_part], axis=2)
    mixed_grad = mixed_grad.astype(LOW).reshape(group_rows, 3 * feats)
    far = against_rows(core_rows(mixed_grad, False), inward_part).astype(LOW)
    near = against_rows(core_rows(mixed_grad, True), inward_part).astype(LOW)
    inward_term = over_tokens(normed_one, mixed_grad).astype(LOW)
    far, near, inward_term, branch_grad_full = together(far, near, inward_term, branch_grad_full)
    inward_column = class_lend(inward_term)
    outward_term = class_pieces(over_tokens(branch_feats, branch_grad_full).astype(LOW))
    from_l, from_x, block = group_lend(near, far)
    from_l, from_x, up_own, inward_column, outward_term = together(
        from_l, from_x, up_own, inward_column, outward_term
    )
    up_own = group_exchange(up_own.reshape(8, d_rows, units))
    inward_own = class_settle(inward_column)
    outward_column = class_lend(outward_term)
    *parts, inward_own, outward_column = together(
        *group_settle(from_l, from_x, block), inward_own, outward_column
    )
    outward_sum = class_settle(outward_column).astype(F32)
    normed_one_grad = rearranged(sum(part.astype(F32) for part in parts), False)
    scale_one, normal_one = rms_parts(inputs)
    input_grad = middle_grad + norm_back(normed_one_grad, normal_one, scale_one, gain_one)

    inward_own = group_exchange(inward_own.reshape(8, d_rows, 3 * feats))

    gate_new, gate_dots = updated_columns(gate_own, gate_weight, gate_first, gate_second, count, 1)
    up_new, up_dots = updated_columns(up_own, up_weight, up_first, up_second, count, 1)
    inward_new, inward_dots = updated_columns(
        inward_own, inward_weight, inward_first, inward_second, count, 3
    )
    own_gains = norm_gains.astype(LOW).astype(F32)
    gain_one_grad = inward_dots / own_gains[0]
    gain_two_grad = (gate_dots + up_dots) / own_gains[1]
    gains_grad = jnp.stack([gain_one_grad, gain_two_grad])
    taps_grad = lax.psum_scatter(tap_grads, CLASS, scatter_dimension=0, tiled=True).T

    outward_new = adamw(
        outward_weight, outward_first, outward_second, outward_sum, RATE_MATRIX, DECAY_RATE
    )
    down_new = adamw(down_weight, down_first, down_second, down_sum, RATE_MATRIX, DECAY_RATE)
    gains_new = adamw(norm_gains, gains_first, gains_second, gains_grad, RATE_VECTOR, 0.0)
    taps_new = adamw(conv_taps, taps_first, taps_second, taps_grad, RATE_VECTOR, 0.0)
    return (
        block_output,
        input_grad,
        *inward_new,
        *outward_new,
        *gate_new,
        *up_new,
        *down_new,
        *gains_new,
        *taps_new,
    )


def solution(mesh):
    devices = mesh.devices.reshape(-1, 2, 2, 2, 2)
    rows = P(AXES, None)
    columns = P(None, AXES)
    return jax.shard_map(
        on_device,
        mesh=Mesh(devices, AXES),
        in_specs=(rows,) * 17 + (columns,) * 6,
        out_specs=(rows,) * 17 + (columns,) * 6,
        check_vma=False,
    )
```

```python
import functools

import jax
import jax.numpy as jnp
from jax import lax
from jax.experimental import pallas as pl
from jax.experimental.pallas import tpu as pltpu
from jax.sharding import Mesh
from jax.sharding import PartitionSpec as P

SEQ_BASE = 8192
STEP = 10

EPS_NORM = 1e-05
BETA_ONE = 0.9
BETA_TWO = 0.95
ADAM_EPS = 1e-08
DECAY_RATE = 0.1
RATE_MATRIX = 0.01
RATE_VECTOR = 0.3

AXES = ("p", "y", "x", "c")
PLANE = ("y", "x", "c")
LOW = jnp.bfloat16
F32 = jnp.float32


def forward_dot(operand, partner):
    return jnp.dot(operand, partner, preferred_element_type=jnp.float32)


def over_tokens(operand, partner):
    return lax.dot_general(
        operand, partner, (((0,), (0,)), ((), ())), preferred_element_type=jnp.float32
    )


def against_rows(operand, partner):
    return lax.dot_general(
        operand, partner, (((1,), (1,)), ((), ())), preferred_element_type=jnp.float32
    )


def rms_parts(values):
    scale = lax.rsqrt(jnp.mean(values * values, axis=-1, keepdims=True) + EPS_NORM)
    return (scale, values * scale)


def norm_back(upstream, normal, scale, gain):
    scaled = upstream * gain
    return scale * (scaled - normal * jnp.mean(scaled * normal, axis=-1, keepdims=True))


def adamw(weight, first, second, grad, rate, decay):
    first_new = BETA_ONE * first + (1.0 - BETA_ONE) * grad
    second_new = BETA_TWO * second + (1.0 - BETA_TWO) * grad * grad
    fix_one = 1.0 - BETA_ONE**STEP
    fix_two = 1.0 - BETA_TWO**STEP
    stepped = first_new / fix_one / (jnp.sqrt(second_new / fix_two) + ADAM_EPS)
    return (first_new, second_new, weight - rate * (stepped + decay * weight))


def after(value, *others):
    return lax.optimization_barrier((value, *others))[0]


def together(*values):
    return lax.optimization_barrier(values)


def swap(block, axis):
    return lax.ppermute(block, axis, [(0, 1), (1, 0)])


def along(block, distance):
    count = lax.axis_size("p")
    route = [(i - distance, i) for i in range(count) if 0 <= i - distance < count]
    return lax.ppermute(block, "p", route)


def over(block, axis):
    other = swap(block, axis)
    first = lax.axis_index(axis) == 0
    return jnp.stack([jnp.where(first, block, other), jnp.where(first, other, block)])


def over_planes(block):
    count = lax.axis_size("p")
    if count > 4:
        return lax.all_gather(block, "p", axis=0, tiled=False)
    pieces = [block]
    for distance in range(1, count):
        route = [((i + distance) % count, i) for i in range(count)]
        pieces.append(lax.ppermute(block, "p", route))
    return jnp.roll(jnp.stack(pieces), lax.axis_index("p"), axis=0)


def plane_blocks(block):
    half = block.shape[0] // 2
    by_x, by_y = swap(block, "x"), swap(block, "y")
    own_far = swap(block, "c")
    corner = jnp.concatenate([swap(by_x[:half], "y"), swap(by_y[half:], "x")], axis=0)
    near = [block, by_x, by_y, corner]
    return near, [own_far] + [swap(piece, "c") for piece in near[1:]]


def plane_gather(block):
    rows = block.shape[0]
    mine_y, mine_x, mine_c = (lax.axis_index(axis) for axis in PLANE)
    out = jnp.zeros((8 * rows, block.shape[1]), block.dtype)
    for dc, pieces in enumerate(plane_blocks(block)):
        for k, piece in enumerate(pieces):
            at = ((mine_y ^ (k >> 1)) * 2 + (mine_x ^ (k & 1))) * 2 + (mine_c ^ dc)
            out = lax.dynamic_update_slice_in_dim(out, piece, at * rows, axis=0)
    return out


def plane_gather_here(block):
    near, far = plane_blocks(block)
    return jnp.concatenate(near + far, axis=0)


def plane_exchange(blocks):
    return lax.all_to_all(blocks, PLANE, split_axis=0, concat_axis=0, tiled=True)


def core_rows(array, own):
    core = lax.axis_index("c") if own else 1 - lax.axis_index("c")
    rows = array.shape[0] // 8
    return jnp.concatenate(
        [lax.dynamic_slice_in_dim(array, (2 * i + core) * rows, rows, axis=0) for i in range(4)],
        axis=0,
    )


def plane_corner(near, got, here=False):
    quarter = near.shape[0] // 4
    half = quarter // 2
    mine_y, mine_x = lax.axis_index("y"), lax.axis_index("x")

    def block(dy, dx):
        if here:
            place = 2 * dy + dx
            return tuple(part[place * quarter : (place + 1) * quarter] for part in (near, got))
        place = (mine_y ^ dy) * 2 + (mine_x ^ dx)
        return tuple(
            lax.dynamic_slice_in_dim(part, place * quarter, quarter, axis=0) for part in (near, got)
        )

    corner = sum(block(1, 1))
    return swap(corner[:half], "y"), swap(corner[half:], "x"), block


def plane_settle(from_y, from_x, block):
    near_x, got_x = block(0, 1)
    near_y, got_y = block(1, 0)
    by_x = near_x + got_x + jnp.concatenate([from_y, jnp.zeros_like(from_y)], axis=0)
    by_y = near_y + got_y + jnp.concatenate([jnp.zeros_like(from_x), from_x], axis=0)
    return sum(block(0, 0)), swap(by_x, "x"), swap(by_y, "y")


def planes_gather(block):
    return lax.all_gather(block, "p", axis=0, tiled=True)


def planes_scatter(term):
    return lax.psum_scatter(term, "p", scatter_dimension=0, tiled=True)


def shifted(block, distance):
    count = lax.axis_size("p")
    return lax.ppermute(block, "p", [((i + distance) % count, i) for i in range(count)])


def planes_gather_small(block):
    count = lax.axis_size("p")
    if count > 4:
        return planes_gather(block)
    pieces = jnp.stack([block] + [shifted(block, i) for i in range(1, count)])
    mine = lax.axis_index("p")
    picked = [
        lax.dynamic_index_in_dim(pieces, (i - mine) % count, axis=0, keepdims=False)
        for i in range(count)
    ]
    return jnp.concatenate(picked, axis=0)


def planes_scatter_small(term):
    count = lax.axis_size("p")
    if count > 4:
        return planes_scatter(term)
    rows = term.shape[0] // count
    mine = lax.axis_index("p")
    total = lax.dynamic_slice_in_dim(term, mine * rows, rows, axis=0).astype(F32)
    for i in range(1, count):
        piece = lax.dynamic_slice_in_dim(term, (mine - i) % count * rows, rows, axis=0)
        total = total + shifted(piece, i).astype(F32)
    return total


def half_body(rows_ref, upstream_ref, both_ref, down_ref, hidden_out, grads_out):
    both = forward_dot(rows_ref[...], both_ref[...])
    half = both.shape[1] // 2
    gate_value, up_value = both[:, :half], both[:, half:]
    sigmoid_gate = jax.nn.sigmoid(gate_value)
    silu_gate = gate_value * sigmoid_gate
    hidden_out[...] = (silu_gate * up_value).astype(LOW)
    hidden_grad = against_rows(upstream_ref[...], down_ref[...])
    gate_grad = hidden_grad * up_value * sigmoid_gate * (1.0 + gate_value * (1.0 - sigmoid_gate))
    grads_out[:, :half] = gate_grad.astype(LOW)
    grads_out[:, half:] = (hidden_grad * silu_gate).astype(LOW)


def half_ffn(rows, upstream, both, down):
    count, d = rows.shape
    half = both.shape[1] // 2
    tile = 512
    return pl.pallas_call(
        half_body,
        grid=(count // tile,),
        in_specs=[
            pl.BlockSpec((tile, d), lambda i: (i, 0)),
            pl.BlockSpec((tile, d), lambda i: (i, 0)),
            pl.BlockSpec(both.shape, lambda i: (0, 0)),
            pl.BlockSpec(down.shape, lambda i: (0, 0)),
        ],
        out_specs=[
            pl.BlockSpec((tile, half), lambda i: (i, 0)),
            pl.BlockSpec((tile, 2 * half), lambda i: (i, 0)),
        ],
        out_shape=[
            jax.ShapeDtypeStruct((count, half), LOW),
            jax.ShapeDtypeStruct((count, 2 * half), LOW),
        ],
        compiler_params=pltpu.CompilerParams(vmem_limit_bytes=48 * 2**20),
        cost_estimate=pl.CostEstimate(
            flops=6 * count * d * half, transcendentals=count * half, bytes_accessed=4 * count * d + 6 * d * half
        ),
    )(rows, upstream, both, down)


def pair_body(turned, a_ref, b_ref, c_ref, e_ref, out_ref):
    dot = against_rows if turned else forward_dot
    out_ref[...] = (dot(a_ref[...], c_ref[...]) + dot(b_ref[...], e_ref[...])).astype(LOW)


def pair_dot(first, second, first_weight, second_weight, far, turned):
    count, depth = first.shape
    width = first_weight.shape[0 if turned else 1]
    tile = 512
    steps = count // 2 // tile
    rows = pl.BlockSpec((tile, depth), lambda i: (i + (steps if far else 0), 0))
    whole = pl.BlockSpec(first_weight.shape, lambda i: (0, 0))
    return pl.pallas_call(
        functools.partial(pair_body, turned),
        grid=(steps,),
        in_specs=[rows, rows, whole, whole],
        out_specs=pl.BlockSpec((tile, width), lambda i: (i, 0)),
        out_shape=jax.ShapeDtypeStruct((count // 2, width), LOW),
        compiler_params=pltpu.CompilerParams(vmem_limit_bytes=48 * 2**20),
        cost_estimate=pl.CostEstimate(
            flops=2 * count * depth * width, transcendentals=0, bytes_accessed=2 * count * (depth + width // 2) + 4 * depth * width
        ),
    )(first, second, first_weight, second_weight)


def pack_body(count, inward_ref, gate_ref, up_ref, inward_out, ffn_out):
    d_rows = inward_ref.shape[1] // (24 * count)
    ff_rows = gate_ref.shape[1] // (8 * count)
    feats, units, width = count * d_rows, count * ff_rows, ff_rows // 2
    for p in range(count):
        for to in range(8):
            at = (p * 8 + to) * ff_rows
            for half in range(2):
                for kind, ref in enumerate((gate_ref, up_ref)):
                    lane = (half * 2 + kind) * units // 2 + p * width
                    block = ref[:, at + half * width : at + (half + 1) * width]
                    ffn_out[to, :, lane : lane + width] = block.astype(LOW)
    for part in range(3):
        for to in range(8):
            blocks = []
            for p in range(count):
                at = ((part * count + p) * 8 + to) * d_rows
                blocks.append(inward_ref[:, at : at + d_rows])
            block = jnp.concatenate(blocks, axis=1).astype(LOW)
            inward_out[to, :, part * feats : (part + 1) * feats] = block


def packed(inward, gate, up, count):
    d_rows, ff = gate.shape
    feats, units = inward.shape[1] // 24, ff // 8
    if d_rows % 64 or units % (256 * count):
        sent = inward.astype(LOW).reshape(d_rows, 3, count, 8, -1)
        sent = sent.transpose(3, 0, 1, 2, 4).reshape(8, d_rows, 3 * feats)
        both = jnp.stack([gate.astype(LOW), up.astype(LOW)], axis=1)
        both = both.reshape(d_rows, 2, count, 8, 2, -1).transpose(3, 0, 4, 1, 2, 5)
        return sent, both.reshape(8, d_rows, 2 * units)
    rows = 16
    return pl.pallas_call(
        functools.partial(pack_body, count),
        grid=(d_rows // rows,),
        in_specs=[
            pl.BlockSpec((rows, 24 * feats), lambda i: (i, 0)),
            pl.BlockSpec((rows, ff), lambda i: (i, 0)),
            pl.BlockSpec((rows, ff), lambda i: (i, 0)),
        ],
        out_specs=[
            pl.BlockSpec((8, rows, 3 * feats), lambda i: (0, i, 0)),
            pl.BlockSpec((8, rows, 2 * units), lambda i: (0, i, 0)),
        ],
        out_shape=[
            jax.ShapeDtypeStruct((8, d_rows, 3 * feats), LOW),
            jax.ShapeDtypeStruct((8, d_rows, 2 * units), LOW),
        ],
        compiler_params=pltpu.CompilerParams(vmem_limit_bytes=32 * 2**20),
        cost_estimate=pl.CostEstimate(
            flops=0, transcendentals=0, bytes_accessed=6 * d_rows * (24 * feats + 2 * ff)
        ),
    )(inward, gate, up)


def update_body(parts, width, pieces, *refs):
    got_refs = refs[:parts]
    weight_ref, first_ref, second_ref, first_out, second_out, weight_out, dot_out = refs[parts:]

    @pl.when(pl.program_id(0) == 0)
    def _():
        dot_out[...] = jnp.zeros_like(dot_out)

    total = jnp.zeros((weight_ref.shape[0], 128), F32)
    joined = 128 // width
    for group in range(0, len(pieces), joined):
        grad = [
            got_refs[which][tuple(at)][:, lane : lane + width].astype(F32)
            for which, *at, lane in pieces[group : group + joined]
        ]
        grad = jnp.concatenate(grad, axis=1) if joined > 1 else grad[0]
        here = slice(group * width, group * width + 128)
        weight = weight_ref[:, here]
        first, second, updated = adamw(
            weight, first_ref[:, here], second_ref[:, here], grad, RATE_MATRIX, DECAY_RATE
        )
        first_out[:, here] = first
        second_out[:, here] = second
        weight_out[:, here] = updated
        total += weight.astype(LOW).astype(F32) * grad
    dot_out[...] += total


def update_call(grid, got, got_specs, width, pieces, weight, first, second):
    rows, columns = weight.shape
    spec = pl.BlockSpec((rows, columns // grid), lambda k: (0, k))
    shape = jax.ShapeDtypeStruct(weight.shape, F32)
    *new, dots = pl.pallas_call(
        functools.partial(update_body, len(got), width, pieces),
        grid=(grid,),
        in_specs=[*got_specs, spec, spec, spec],
        out_specs=[spec, spec, spec, pl.BlockSpec((rows, 128), lambda k: (0, 0))],
        out_shape=[shape, shape, shape, jax.ShapeDtypeStruct((rows, 128), F32)],
        compiler_params=pltpu.CompilerParams(vmem_limit_bytes=32 * 2**20),
        cost_estimate=pl.CostEstimate(
            flops=20 * rows * columns, transcendentals=2 * rows * columns, bytes_accessed=26 * rows * columns
        ),
    )(*got, weight, first, second)
    return tuple(new), jnp.sum(dots, axis=1)


def updated_plainly(grad, weight, first, second):
    grad = grad.reshape(weight.shape).astype(F32)
    new = adamw(weight, first, second, grad, RATE_MATRIX, DECAY_RATE)
    return new, jnp.sum(weight.astype(LOW).astype(F32) * grad, axis=1)


def updated_inward(got, weight, first, second, count):
    rows, columns = weight.shape
    width = columns // (24 * count)
    if width % 64 or rows % 16:
        grad = got.reshape(8, rows, 3, count, width).transpose(1, 2, 3, 0, 4)
        return updated_plainly(grad, weight, first, second)
    spec = pl.BlockSpec((8, rows, count * width), lambda k: (0, 0, k))
    pieces = [(0, to, p * width) for p in range(count) for to in range(8)]
    return update_call(3, [got], [spec], width, pieces, weight, first, second)


def updated_ffn(got, kind, weight, first, second, count):
    rows, columns = weight.shape
    width = columns // (16 * count)
    if width % 128 or rows % 16:
        grad = jnp.stack(got).reshape(2, 8, rows, 2, count, width)[:, :, :, kind]
        return updated_plainly(grad.transpose(2, 3, 1, 0, 4), weight, first, second)
    spec = pl.BlockSpec((4, rows, width), lambda k: (k % 2, 0, kind * count + k // 2))
    pieces = [
        (half, q, lane) for q in range(4) for half in range(2) for lane in range(0, width, 128)
    ]
    return update_call(2 * count, got, [spec, spec], 128, pieces, weight, first, second)


def on_device(
    block_input,
    cotangent,
    inward_weight,
    inward_first,
    inward_second,
    outward_weight,
    outward_first,
    outward_second,
    gate_weight,
    gate_first,
    gate_second,
    up_weight,
    up_first,
    up_second,
    down_weight,
    down_first,
    down_second,
    norm_gains,
    gains_first,
    gains_second,
    conv_taps,
    taps_first,
    taps_second,
):
    count = lax.axis_size("p")
    tok_rows, d = block_input.shape
    d_rows = inward_weight.shape[0]
    ff = gate_weight.shape[1]
    ff_rows = down_weight.shape[0]
    plane_rows = 8 * tok_rows
    near_rows = 4 * tok_rows
    seq_len = min(SEQ_BASE, plane_rows * count)
    feats = d // 8
    units = ff // 8
    half = units // 2
    place = lax.axis_index(PLANE)

    down_low = down_weight.astype(LOW)
    block_here, outward_here, small = together(
        block_input, outward_weight, jnp.concatenate([norm_gains, conv_taps], axis=0), down_low
    )[:3]
    outward_low = outward_here.astype(LOW)
    down_a, down_b = down_low[: ff_rows // 2], down_low[ff_rows // 2 :]
    down_parts = [planes_gather(down_a)]
    inward_sent, ffn_sent = packed(after(inward_weight, down_low), gate_weight, up_weight, count)
    inward_got = plane_exchange(inward_sent).reshape(8 * d_rows, 3 * feats)
    inward_got, first_down = together(inward_got, down_parts[0])
    down_parts = [first_down]
    inward_part = planes_gather(inward_got)
    ffn_got = plane_exchange(after(ffn_sent, inward_got)).reshape(8 * d_rows, 2 * units)
    ffn_parts = [planes_gather(ffn_got[:, :units])]
    inputs_low = plane_gather(block_here)
    small = over(over(over(over_planes(small.astype(LOW)), "c"), "x"), "y").transpose(3, 0, 1, 2, 4, 5)
    outward_part = planes_gather_small(outward_low)
    inputs_low, small, outward_part, ffn_got = together(inputs_low, small, outward_part, ffn_got)
    upstream = plane_gather_here(after(cotangent, inputs_low))
    outward_full = plane_gather(after(outward_part, upstream))
    small = small.astype(F32)
    gain_one = small[..., 0, :].reshape(d)
    gain_two = small[..., 1, :].reshape(d)
    taps_here = lax.dynamic_index_in_dim(
        small.reshape(count, 8, 5, d_rows), place, axis=1, keepdims=False
    )
    taps_here = taps_here[:, 2:].transpose(1, 0, 2).reshape(3, feats)
    tap_zero, tap_one, tap_two = taps_here[0], taps_here[1], taps_here[2]

    _, normed_one = rms_parts(inputs_low.astype(F32))
    normed_one = (normed_one * gain_one).astype(LOW)
    mixed = forward_dot(normed_one, inward_part)
    b_part = mixed[:, :feats]
    c_part = mixed[:, feats : 2 * feats]
    x_part = mixed[:, 2 * feats :]
    gated = b_part * x_part
    starts_here = lax.axis_index("p") * plane_rows % seq_len == 0
    before = jnp.where(starts_here, 0.0, along(gated[plane_rows - 2 :], 1))
    extended = jnp.concatenate([before, gated], axis=0)
    convolved = (
        tap_zero * extended[:plane_rows]
        + tap_one * extended[1 : plane_rows + 1]
        + tap_two * extended[2:]
    )
    branch_feats = (c_part * convolved).astype(LOW)
    branch_got = plane_exchange(branch_feats.reshape(8, tok_rows, feats))
    branch_in = branch_got.transpose(1, 0, 2).reshape(tok_rows, d)
    branch_in, down_b, ffn_b = together(branch_in, down_b, ffn_got[:, units:])
    down_parts += [planes_gather(down_b)]
    ffn_parts += [planes_gather(ffn_b)]
    inputs = block_input.astype(F32)
    middle = inputs + forward_dot(branch_in, outward_full)
    scale_two, normal_two = rms_parts(middle)
    normed_two = plane_gather_here((normal_two * gain_two).astype(LOW))

    def terms_of(hidden, grads):
        return over_tokens(hidden, upstream).astype(LOW), over_tokens(normed_two, grads).astype(LOW)

    hidden_a, grads_a = half_ffn(normed_two, upstream, ffn_parts[0], down_parts[0])
    down_term, both_term = terms_of(hidden_a, grads_a)
    down_own, both_own = [planes_scatter(down_term)], [planes_scatter(both_term)]
    ffn_b, down_b, _, _ = together(ffn_parts[1], down_parts[1], down_term, both_term)
    hidden_b, grads_b = half_ffn(normed_two, upstream, ffn_b, down_b)
    far = pair_dot(grads_a, grads_b, ffn_parts[0], ffn_b, True, True)
    got = swap(far, "c")
    near = pair_dot(grads_a, grads_b, ffn_parts[0], ffn_b, False, True)
    got, near, hidden_b, grads_b = together(got, near, hidden_b, grads_b)
    from_y, from_x, block = plane_corner(near, got, True)
    both_term = over_tokens(normed_two, grads_b).astype(LOW)
    from_y, from_x, both_term = together(from_y, from_x, both_term)
    both_own += [planes_scatter(both_term)]
    down_term = over_tokens(hidden_b, upstream).astype(LOW)
    result_far = pair_dot(hidden_a, hidden_b, down_parts[0], down_b, True, False)
    *parts, down_term, result_far = together(
        *plane_settle(from_y, from_x, block), down_term, result_far
    )
    normed_two_grad = sum(part.astype(F32) for part in parts)

    result_got = swap(result_far, "c")
    result_near = pair_dot(hidden_a, hidden_b, down_parts[0], down_b, False, False)
    middle_grad = cotangent.astype(F32) + norm_back(
        normed_two_grad, normal_two, scale_two, gain_two
    )
    branch_grad = middle_grad.astype(LOW)
    branch_in_grad = against_rows(branch_grad, outward_full).astype(LOW)

    def outward_rows(own):
        core = lax.axis_index("c") if own else 1 - lax.axis_index("c")
        split = branch_got.reshape(4, 2, tok_rows, feats)
        part = lax.dynamic_index_in_dim(split, core, axis=1, keepdims=False)
        term = lax.dot_general(
            part, branch_grad, (((1,), (0,)), ((), ())), preferred_element_type=jnp.float32
        )
        return term.astype(LOW).reshape(d // 2, d)

    outward_far = outward_rows(False)
    branch_in_grad, result_got, result_near, outward_far = together(
        branch_in_grad, result_got, result_near, outward_far
    )
    branch_in_grad = plane_exchange(branch_in_grad.reshape(tok_rows, 8, feats).transpose(1, 0, 2))
    result_y, result_x, result_block = plane_corner(result_near, result_got, True)
    outward_got, outward_near = swap(outward_far, "c"), outward_rows(True)
    branch_in_grad, result_y, result_x, outward_got, outward_near = together(
        branch_in_grad, result_y, result_x, outward_got, outward_near
    )
    result_parts = plane_settle(result_y, result_x, result_block)
    outward_y, outward_x, outward_block = plane_corner(outward_near, outward_got)
    branch_in_grad = branch_in_grad.reshape(plane_rows, feats).astype(F32)
    c_grad = branch_in_grad * convolved
    conv_grad = branch_in_grad * c_part
    ext_grad = (
        jnp.pad(tap_zero * conv_grad, ((0, 2), (0, 0)))
        + jnp.pad(tap_one * conv_grad, ((1, 1), (0, 0)))
        + jnp.pad(tap_two * conv_grad, ((2, 0), (0, 0)))
    )
    tap_grads = jnp.stack(
        [
            jnp.sum(conv_grad * extended[offset : offset + plane_rows], axis=0)
            for offset in range(3)
        ],
        axis=1,
    )
    returned = along(jnp.where(starts_here, 0.0, ext_grad[:2]), -1)
    gated_grad = ext_grad[2:] + jnp.pad(returned, ((plane_rows - 2, 0), (0, 0)))
    mixed_grad = jnp.concatenate([gated_grad * x_part, c_grad, gated_grad * b_part], axis=1)
    mixed_grad = mixed_grad.astype(LOW)
    inward_term = over_tokens(normed_one, mixed_grad).astype(LOW)
    inward_term, mixed_grad, outward_y, outward_x, down_own[0], both_own[0], *result_parts = together(
        inward_term, mixed_grad, outward_y, outward_x, down_own[0], both_own[0], *result_parts
    )
    inward_own = planes_scatter(inward_term)
    block_output = (middle + sum(part.astype(F32) for part in result_parts)).astype(LOW)
    outward_parts = plane_settle(outward_y, outward_x, outward_block)
    far = against_rows(core_rows(mixed_grad, False), inward_part).astype(LOW)
    got = swap(far, "c")
    near = against_rows(core_rows(mixed_grad, True), inward_part).astype(LOW)
    got, near, both_own[1], *outward_parts = together(got, near, both_own[1], *outward_parts)
    outward_own = sum(part.astype(F32) for part in outward_parts).astype(LOW)
    from_y, from_x, block = plane_corner(near, got)
    from_y, from_x = together(from_y, from_x)
    parts = plane_settle(from_y, from_x, block)
    down_own += [planes_scatter(after(down_term, inward_own))]
    normed_one_grad = sum(part.astype(F32) for part in parts)
    scale_one, normal_one = rms_parts(inputs)
    input_grad = middle_grad + norm_back(normed_one_grad, normal_one, scale_one, gain_one)

    outward_sum = planes_scatter_small(outward_own).astype(F32)

    both_got = [plane_exchange(own.reshape(8, d_rows, units)) for own in both_own]
    down_sum = jnp.concatenate(down_own, axis=0).astype(F32)
    inward_own = plane_exchange(inward_own.reshape(8, d_rows, 3 * feats))

    gate_new, gate_dots = updated_ffn(both_got, 0, gate_weight, gate_first, gate_second, count)
    up_new, up_dots = updated_ffn(both_got, 1, up_weight, up_first, up_second, count)
    inward_new, inward_dots = updated_inward(
        inward_own, inward_weight, inward_first, inward_second, count
    )
    own_gains = norm_gains.astype(LOW).astype(F32)
    gain_one_grad = inward_dots / own_gains[0]
    gain_two_grad = (gate_dots + up_dots) / own_gains[1]
    gains_grad = jnp.stack([gain_one_grad, gain_two_grad])
    taps_grad = planes_scatter_small(tap_grads).T

    outward_new = adamw(
        outward_weight, outward_first, outward_second, outward_sum, RATE_MATRIX, DECAY_RATE
    )
    down_new = adamw(down_weight, down_first, down_second, down_sum, RATE_MATRIX, DECAY_RATE)
    gains_new = adamw(norm_gains, gains_first, gains_second, gains_grad, RATE_VECTOR, 0.0)
    taps_new = adamw(conv_taps, taps_first, taps_second, taps_grad, RATE_VECTOR, 0.0)
    return (
        block_output,
        input_grad,
        *inward_new,
        *outward_new,
        *gate_new,
        *up_new,
        *down_new,
        *gains_new,
        *taps_new,
    )


def solution(mesh):
    devices = mesh.devices.reshape(-1, 2, 2, 2)
    rows = P(AXES, None)
    columns = P(None, AXES)
    return jax.shard_map(
        on_device,
        mesh=Mesh(devices, AXES),
        in_specs=(rows,) * 17 + (columns,) * 6,
        out_specs=(rows,) * 17 + (columns,) * 6,
        check_vma=False,
    )
```

```python
import functools

import jax
import jax.numpy as jnp
from jax import lax
from jax.experimental import pallas as pl
from jax.experimental.pallas import tpu as pltpu
from jax.sharding import Mesh
from jax.sharding import PartitionSpec as P

SEQ_BASE = 8192
STEP = 10

EPS_NORM = 1e-05
BETA_ONE = 0.9
BETA_TWO = 0.95
ADAM_EPS = 1e-08
DECAY_RATE = 0.1
RATE_MATRIX = 0.01
RATE_VECTOR = 0.3

AXES = ("p", "y", "x", "c")
PLANE = ("y", "x", "c")
LOW = jnp.bfloat16
F32 = jnp.float32


def forward_dot(operand, partner):
    return jnp.dot(operand, partner, preferred_element_type=jnp.float32)


def over_tokens(operand, partner):
    return lax.dot_general(
        operand, partner, (((0,), (0,)), ((), ())), preferred_element_type=jnp.float32
    )


def against_rows(operand, partner):
    return lax.dot_general(
        operand, partner, (((1,), (1,)), ((), ())), preferred_element_type=jnp.float32
    )


def rms_parts(values):
    scale = lax.rsqrt(jnp.mean(values * values, axis=-1, keepdims=True) + EPS_NORM)
    return (scale, values * scale)


def norm_back(upstream, normal, scale, gain):
    scaled = upstream * gain
    return scale * (scaled - normal * jnp.mean(scaled * normal, axis=-1, keepdims=True))


def adamw(weight, first, second, grad, rate, decay):
    first_new = BETA_ONE * first + (1.0 - BETA_ONE) * grad
    second_new = BETA_TWO * second + (1.0 - BETA_TWO) * grad * grad
    fix_one = 1.0 - BETA_ONE**STEP
    fix_two = 1.0 - BETA_TWO**STEP
    stepped = first_new / fix_one / (jnp.sqrt(second_new / fix_two) + ADAM_EPS)
    return (first_new, second_new, weight - rate * (stepped + decay * weight))


def after(value, *others):
    return lax.optimization_barrier((value, *others))[0]


def together(*values):
    return lax.optimization_barrier(values)


def swap(block, axis):
    return lax.ppermute(block, axis, [(0, 1), (1, 0)])


def along(block, distance):
    count = lax.axis_size("p")
    route = [(i - distance, i) for i in range(count) if 0 <= i - distance < count]
    return lax.ppermute(block, "p", route)


def over(block, axis):
    other = swap(block, axis)
    first = lax.axis_index(axis) == 0
    return jnp.stack([jnp.where(first, block, other), jnp.where(first, other, block)])


def plane_near(block):
    return block, swap(block, "x"), swap(block, "y"), swap(block, "c")


def plane_blocks(block, by_x=None, by_y=None, own_far=None):
    if by_x is None:
        block, by_x, by_y, own_far = plane_near(block)
    half = block.shape[0] // 2
    corner = jnp.concatenate([swap(by_x[:half], "y"), swap(by_y[half:], "x")], axis=0)
    near = [block, by_x, by_y, corner]
    return near, [own_far] + [swap(piece, "c") for piece in near[1:]]


def plane_gather(block, *near):
    rows = block.shape[0]
    mine_y, mine_x, mine_c = (lax.axis_index(axis) for axis in PLANE)
    out = jnp.zeros((8 * rows, block.shape[1]), block.dtype)
    for dc, pieces in enumerate(plane_blocks(block, *near)):
        for k, piece in enumerate(pieces):
            at = ((mine_y ^ (k >> 1)) * 2 + (mine_x ^ (k & 1))) * 2 + (mine_c ^ dc)
            out = lax.dynamic_update_slice_in_dim(out, piece, at * rows, axis=0)
    return out


def plane_gather_here(block):
    near, far = plane_blocks(block)
    return jnp.concatenate(near + far, axis=0)


def plane_exchange(blocks):
    return lax.all_to_all(blocks, PLANE, split_axis=0, concat_axis=0, tiled=True)


def core_rows(array, own):
    core = lax.axis_index("c") if own else 1 - lax.axis_index("c")
    rows = array.shape[0] // 8
    return jnp.concatenate(
        [lax.dynamic_slice_in_dim(array, (2 * i + core) * rows, rows, axis=0) for i in range(4)],
        axis=0,
    )


def plane_corner(near, got, here=False):
    quarter = near.shape[0] // 4
    half = quarter // 2
    mine_y, mine_x = lax.axis_index("y"), lax.axis_index("x")

    def block(dy, dx):
        if here:
            place = 2 * dy + dx
            return tuple(part[place * quarter : (place + 1) * quarter] for part in (near, got))
        place = (mine_y ^ dy) * 2 + (mine_x ^ dx)
        return tuple(
            lax.dynamic_slice_in_dim(part, place * quarter, quarter, axis=0) for part in (near, got)
        )

    corner = sum(block(1, 1))
    return swap(corner[:half], "y"), swap(corner[half:], "x"), block


def plane_settle(from_y, from_x, block):
    near_x, got_x = block(0, 1)
    near_y, got_y = block(1, 0)
    by_x = near_x + got_x + jnp.concatenate([from_y, jnp.zeros_like(from_y)], axis=0)
    by_y = near_y + got_y + jnp.concatenate([jnp.zeros_like(from_x), from_x], axis=0)
    return sum(block(0, 0)), swap(by_x, "x"), swap(by_y, "y")


def planes_gather(block):
    return lax.all_gather(block, "p", axis=0, tiled=True)


def planes_scatter(term):
    return lax.psum_scatter(term, "p", scatter_dimension=0, tiled=True)


def shifted(block, distance):
    count = lax.axis_size("p")
    return lax.ppermute(block, "p", [((i + distance) % count, i) for i in range(count)])


def planes_scatter_small(term):
    count = lax.axis_size("p")
    if count > 4:
        return [planes_scatter(term)]
    rows = term.shape[0] // count
    mine = lax.axis_index("p")
    parts = [lax.dynamic_slice_in_dim(term, mine * rows, rows, axis=0)]
    for i in range(1, count):
        piece = lax.dynamic_slice_in_dim(term, (mine - i) % count * rows, rows, axis=0)
        parts.append(shifted(piece, i))
    return parts


def half_body(rows_ref, upstream_ref, both_ref, down_ref, hidden_out, grads_out):
    both = forward_dot(rows_ref[...], both_ref[...])
    half = both.shape[1] // 2
    gate_value, up_value = both[:, :half], both[:, half:]
    sigmoid_gate = jax.nn.sigmoid(gate_value)
    silu_gate = gate_value * sigmoid_gate
    hidden_out[...] = (silu_gate * up_value).astype(LOW)
    hidden_grad = against_rows(upstream_ref[...], down_ref[...])
    gate_grad = hidden_grad * up_value * sigmoid_gate * (1.0 + gate_value * (1.0 - sigmoid_gate))
    grads_out[:, :half] = gate_grad.astype(LOW)
    grads_out[:, half:] = (hidden_grad * silu_gate).astype(LOW)


def half_ffn(rows, upstream, both, down):
    count, d = rows.shape
    half = both.shape[1] // 2
    tile = 512
    return pl.pallas_call(
        half_body,
        grid=(count // tile,),
        in_specs=[
            pl.BlockSpec((tile, d), lambda i: (i, 0)),
            pl.BlockSpec((tile, d), lambda i: (i, 0)),
            pl.BlockSpec(both.shape, lambda i: (0, 0)),
            pl.BlockSpec(down.shape, lambda i: (0, 0)),
        ],
        out_specs=[
            pl.BlockSpec((tile, half), lambda i: (i, 0)),
            pl.BlockSpec((tile, 2 * half), lambda i: (i, 0)),
        ],
        out_shape=[
            jax.ShapeDtypeStruct((count, half), LOW),
            jax.ShapeDtypeStruct((count, 2 * half), LOW),
        ],
        compiler_params=pltpu.CompilerParams(vmem_limit_bytes=48 * 2**20),
        cost_estimate=pl.CostEstimate(
            flops=6 * count * d * half, transcendentals=count * half, bytes_accessed=4 * count * d + 6 * d * half
        ),
    )(rows, upstream, both, down)


def pair_body(turned, a_ref, b_ref, c_ref, e_ref, out_ref):
    dot = against_rows if turned else forward_dot
    out_ref[...] = (dot(a_ref[...], c_ref[...]) + dot(b_ref[...], e_ref[...])).astype(LOW)


def pair_dot(first, second, first_weight, second_weight, far, turned):
    count, depth = first.shape
    width = first_weight.shape[0 if turned else 1]
    tile = 512
    steps = count // 2 // tile
    rows = pl.BlockSpec((tile, depth), lambda i: (i + (steps if far else 0), 0))
    whole = pl.BlockSpec(first_weight.shape, lambda i: (0, 0))
    return pl.pallas_call(
        functools.partial(pair_body, turned),
        grid=(steps,),
        in_specs=[rows, rows, whole, whole],
        out_specs=pl.BlockSpec((tile, width), lambda i: (i, 0)),
        out_shape=jax.ShapeDtypeStruct((count // 2, width), LOW),
        compiler_params=pltpu.CompilerParams(vmem_limit_bytes=48 * 2**20),
        cost_estimate=pl.CostEstimate(
            flops=2 * count * depth * width, transcendentals=0, bytes_accessed=2 * count * (depth + width // 2) + 4 * depth * width
        ),
    )(first, second, first_weight, second_weight)


def pack_body(count, inward_ref, gate_ref, up_ref, inward_out, ffn_out):
    d_rows = inward_ref.shape[1] // (24 * count)
    ff_rows = gate_ref.shape[1] // (8 * count)
    feats, units, width = count * d_rows, count * ff_rows, ff_rows // 2
    for p in range(count):
        for to in range(8):
            at = (p * 8 + to) * ff_rows
            for half in range(2):
                for kind, ref in enumerate((gate_ref, up_ref)):
                    lane = (half * 2 + kind) * units // 2 + p * width
                    block = ref[:, at + half * width : at + (half + 1) * width]
                    ffn_out[to, :, lane : lane + width] = block.astype(LOW)
    for part in range(3):
        for to in range(8):
            blocks = []
            for p in range(count):
                at = ((part * count + p) * 8 + to) * d_rows
                blocks.append(inward_ref[:, at : at + d_rows])
            block = jnp.concatenate(blocks, axis=1).astype(LOW)
            inward_out[to, :, part * feats : (part + 1) * feats] = block


def packed(inward, gate, up, count):
    d_rows, ff = gate.shape
    feats, units = inward.shape[1] // 24, ff // 8
    if d_rows % 64 or units % (256 * count):
        sent = inward.astype(LOW).reshape(d_rows, 3, count, 8, -1)
        sent = sent.transpose(3, 0, 1, 2, 4).reshape(8, d_rows, 3 * feats)
        both = jnp.stack([gate.astype(LOW), up.astype(LOW)], axis=1)
        both = both.reshape(d_rows, 2, count, 8, 2, -1).transpose(3, 0, 4, 1, 2, 5)
        return sent, both.reshape(8, d_rows, 2 * units)
    rows = 16
    return pl.pallas_call(
        functools.partial(pack_body, count),
        grid=(d_rows // rows,),
        in_specs=[
            pl.BlockSpec((rows, 24 * feats), lambda i: (i, 0)),
            pl.BlockSpec((rows, ff), lambda i: (i, 0)),
            pl.BlockSpec((rows, ff), lambda i: (i, 0)),
        ],
        out_specs=[
            pl.BlockSpec((8, rows, 3 * feats), lambda i: (0, i, 0)),
            pl.BlockSpec((8, rows, 2 * units), lambda i: (0, i, 0)),
        ],
        out_shape=[
            jax.ShapeDtypeStruct((8, d_rows, 3 * feats), LOW),
            jax.ShapeDtypeStruct((8, d_rows, 2 * units), LOW),
        ],
        compiler_params=pltpu.CompilerParams(vmem_limit_bytes=32 * 2**20),
        cost_estimate=pl.CostEstimate(
            flops=0, transcendentals=0, bytes_accessed=6 * d_rows * (24 * feats + 2 * ff)
        ),
    )(inward, gate, up)


def update_body(parts, width, pieces, *refs):
    got_refs = refs[:parts]
    weight_ref, first_ref, second_ref, first_out, second_out, weight_out, dot_out = refs[parts:]

    @pl.when(pl.program_id(0) == 0)
    def _():
        dot_out[...] = jnp.zeros_like(dot_out)

    total = jnp.zeros((weight_ref.shape[0], 128), F32)
    joined = 128 // width
    for group in range(0, len(pieces), joined):
        grad = [
            got_refs[which][tuple(at)][:, lane : lane + width].astype(F32)
            for which, *at, lane in pieces[group : group + joined]
        ]
        grad = jnp.concatenate(grad, axis=1) if joined > 1 else grad[0]
        here = slice(group * width, group * width + 128)
        weight = weight_ref[:, here]
        first, second, updated = adamw(
            weight, first_ref[:, here], second_ref[:, here], grad, RATE_MATRIX, DECAY_RATE
        )
        first_out[:, here] = first
        second_out[:, here] = second
        weight_out[:, here] = updated
        total += weight.astype(LOW).astype(F32) * grad
    dot_out[...] += total


def update_call(grid, got, got_specs, width, pieces, weight, first, second):
    rows, columns = weight.shape
    spec = pl.BlockSpec((rows, columns // grid), lambda k: (0, k))
    shape = jax.ShapeDtypeStruct(weight.shape, F32)
    *new, dots = pl.pallas_call(
        functools.partial(update_body, len(got), width, pieces),
        grid=(grid,),
        in_specs=[*got_specs, spec, spec, spec],
        out_specs=[spec, spec, spec, pl.BlockSpec((rows, 128), lambda k: (0, 0))],
        out_shape=[shape, shape, shape, jax.ShapeDtypeStruct((rows, 128), F32)],
        compiler_params=pltpu.CompilerParams(vmem_limit_bytes=32 * 2**20),
        cost_estimate=pl.CostEstimate(
            flops=20 * rows * columns, transcendentals=2 * rows * columns, bytes_accessed=26 * rows * columns
        ),
    )(*got, weight, first, second)
    return tuple(new), jnp.sum(dots, axis=1)


def updated_plainly(grad, weight, first, second):
    grad = grad.reshape(weight.shape).astype(F32)
    new = adamw(weight, first, second, grad, RATE_MATRIX, DECAY_RATE)
    return new, jnp.sum(weight.astype(LOW).astype(F32) * grad, axis=1)


def updated_inward(got, weight, first, second, count):
    rows, columns = weight.shape
    width = columns // (24 * count)
    if width % 64 or rows % 16:
        grad = got.reshape(8, rows, 3, count, width).transpose(1, 2, 3, 0, 4)
        return updated_plainly(grad, weight, first, second)
    spec = pl.BlockSpec((8, rows, count * width), lambda k: (0, 0, k))
    pieces = [(0, to, p * width) for p in range(count) for to in range(8)]
    return update_call(3, [got], [spec], width, pieces, weight, first, second)


def updated_ffn(got, kind, weight, first, second, count):
    rows, columns = weight.shape
    width = columns // (16 * count)
    if width % 128 or rows % 16:
        grad = jnp.stack(got).reshape(2, 8, rows, 2, count, width)[:, :, :, kind]
        return updated_plainly(grad.transpose(2, 3, 1, 0, 4), weight, first, second)
    spec = pl.BlockSpec((4, rows, width), lambda k: (k % 2, 0, kind * count + k // 2))
    pieces = [
        (half, q, lane) for q in range(4) for half in range(2) for lane in range(0, width, 128)
    ]
    return update_call(2 * count, got, [spec, spec], 128, pieces, weight, first, second)


def on_device(
    block_input,
    cotangent,
    inward_weight,
    inward_first,
    inward_second,
    outward_weight,
    outward_first,
    outward_second,
    gate_weight,
    gate_first,
    gate_second,
    up_weight,
    up_first,
    up_second,
    down_weight,
    down_first,
    down_second,
    norm_gains,
    gains_first,
    gains_second,
    conv_taps,
    taps_first,
    taps_second,
):
    count = lax.axis_size("p")
    tok_rows, d = block_input.shape
    d_rows = inward_weight.shape[0]
    ff = gate_weight.shape[1]
    ff_rows = down_weight.shape[0]
    plane_rows = 8 * tok_rows
    near_rows = 4 * tok_rows
    seq_len = min(SEQ_BASE, plane_rows * count)
    feats = d // 8
    units = ff // 8
    half = units // 2
    place = lax.axis_index(PLANE)

    down_low = down_weight.astype(LOW)
    down_a, down_b = down_low[: ff_rows // 2], down_low[ff_rows // 2 :]
    small = jnp.concatenate([norm_gains, conv_taps], axis=0).astype(LOW)
    small = jnp.pad(small, ((0, 11), (0, d - d_rows)))
    first = jnp.concatenate([down_a, outward_weight.astype(LOW), small], axis=0)
    first_part = planes_gather(first)
    block_here, inward_here, _ = together(block_input, inward_weight, first)
    inward_sent, ffn_sent = packed(inward_here, gate_weight, up_weight, count)
    inward_got = plane_exchange(inward_sent).reshape(8 * d_rows, 3 * feats)
    ffn_got = plane_exchange(after(ffn_sent, inward_got)).reshape(8 * d_rows, 2 * units)
    *inputs_near, inward_got, ffn_got, first_part = together(
        *plane_near(block_here), inward_got, ffn_got, first_part
    )
    inward_part = planes_gather(inward_got)
    ffn_parts = [planes_gather(ffn_got[:, :units]), planes_gather(ffn_got[:, units:])]
    first_part = first_part.reshape(count, -1, d)
    down_parts = [first_part[:, : ff_rows // 2].reshape(-1, d), planes_gather(down_b)]
    outward_part = first_part[:, ff_rows // 2 : ff_rows // 2 + d_rows].reshape(-1, d)
    small = first_part[:, ff_rows // 2 + d_rows :][:, :5, :d_rows]
    small = over(over(over(small, "c"), "x"), "y").transpose(3, 0, 1, 2, 4, 5)
    inputs_low = plane_gather(*inputs_near)
    inputs_low, small, outward_part = together(inputs_low, small, outward_part)
    outward_full = plane_gather(outward_part)
    small = small.astype(F32)
    gain_one = small[..., 0, :].reshape(d)
    gain_two = small[..., 1, :].reshape(d)
    taps_here = lax.dynamic_index_in_dim(
        small.reshape(count, 8, 5, d_rows), place, axis=1, keepdims=False
    )
    taps_here = taps_here[:, 2:].transpose(1, 0, 2).reshape(3, feats)
    tap_zero, tap_one, tap_two = taps_here[0], taps_here[1], taps_here[2]

    _, normed_one = rms_parts(inputs_low.astype(F32))
    normed_one = (normed_one * gain_one).astype(LOW)
    mixed = forward_dot(normed_one, inward_part)
    mixed, cotangent_here = together(mixed, cotangent)
    upstream = plane_gather_here(cotangent_here)
    b_part = mixed[:, :feats]
    c_part = mixed[:, feats : 2 * feats]
    x_part = mixed[:, 2 * feats :]
    gated = b_part * x_part
    starts_here = lax.axis_index("p") * plane_rows % seq_len == 0
    before = jnp.where(starts_here, 0.0, along(gated[plane_rows - 2 :], 1))
    extended = jnp.concatenate([before, gated], axis=0)
    convolved = (
        tap_zero * extended[:plane_rows]
        + tap_one * extended[1 : plane_rows + 1]
        + tap_two * extended[2:]
    )
    branch_feats = (c_part * convolved).astype(LOW)
    branch_got = plane_exchange(branch_feats.reshape(8, tok_rows, feats))
    branch_in = branch_got.transpose(1, 0, 2).reshape(tok_rows, d)
    branch_in, upstream = together(branch_in, upstream)
    inputs = block_input.astype(F32)
    middle = inputs + forward_dot(branch_in, outward_full)
    scale_two, normal_two = rms_parts(middle)
    normed_two = plane_gather_here((normal_two * gain_two).astype(LOW))

    def terms_of(hidden, grads):
        return over_tokens(hidden, upstream).astype(LOW), over_tokens(normed_two, grads).astype(LOW)

    hidden_a, grads_a = half_ffn(normed_two, upstream, ffn_parts[0], down_parts[0])
    down_term, both_term = terms_of(hidden_a, grads_a)
    down_own, both_own = [planes_scatter(down_term)], [planes_scatter(both_term)]
    ffn_b, down_b, _, _ = together(ffn_parts[1], down_parts[1], down_term, both_term)
    hidden_b, grads_b = half_ffn(normed_two, upstream, ffn_b, down_b)
    far = pair_dot(grads_a, grads_b, ffn_parts[0], ffn_b, True, True)
    got = swap(far, "c")
    near = pair_dot(grads_a, grads_b, ffn_parts[0], ffn_b, False, True)
    got, near, hidden_b, grads_b = together(got, near, hidden_b, grads_b)
    from_y, from_x, block = plane_corner(near, got, True)
    both_term = over_tokens(normed_two, grads_b).astype(LOW)
    from_y, from_x, both_term = together(from_y, from_x, both_term)
    both_own += [planes_scatter(both_term)]
    down_term = over_tokens(hidden_b, upstream).astype(LOW)
    result_far = pair_dot(hidden_a, hidden_b, down_parts[0], down_b, True, False)
    result_near = pair_dot(hidden_a, hidden_b, down_parts[0], down_b, False, False)
    *parts, down_term, result_far, result_near = together(
        *plane_settle(from_y, from_x, block), down_term, result_far, result_near
    )
    normed_two_grad = sum(part.astype(F32) for part in parts)

    result_got = swap(result_far, "c")
    middle_grad = cotangent.astype(F32) + norm_back(
        normed_two_grad, normal_two, scale_two, gain_two
    )
    branch_grad = middle_grad.astype(LOW)
    branch_in_grad = against_rows(branch_grad, outward_full).astype(LOW)

    def outward_rows(own):
        core = lax.axis_index("c") if own else 1 - lax.axis_index("c")
        split = branch_got.reshape(4, 2, tok_rows, feats)
        part = lax.dynamic_index_in_dim(split, core, axis=1, keepdims=False)
        term = lax.dot_general(
            part, branch_grad, (((1,), (0,)), ((), ())), preferred_element_type=jnp.float32
        )
        return term.astype(LOW).reshape(d // 2, d)

    outward_far = outward_rows(False)
    branch_in_grad, result_got, result_near, outward_far = together(
        branch_in_grad, result_got, result_near, outward_far
    )
    branch_in_grad = plane_exchange(branch_in_grad.reshape(tok_rows, 8, feats).transpose(1, 0, 2))
    result_y, result_x, result_block = plane_corner(result_near, result_got, True)
    outward_got, outward_near = swap(outward_far, "c"), outward_rows(True)
    branch_in_grad, outward_got, outward_near = together(branch_in_grad, outward_got, outward_near)
    branch_in_grad = branch_in_grad.reshape(plane_rows, feats).astype(F32)
    c_grad = branch_in_grad * convolved
    conv_grad = branch_in_grad * c_part
    ext_grad = (
        jnp.pad(tap_zero * conv_grad, ((0, 2), (0, 0)))
        + jnp.pad(tap_one * conv_grad, ((1, 1), (0, 0)))
        + jnp.pad(tap_two * conv_grad, ((2, 0), (0, 0)))
    )
    tap_grads = jnp.stack(
        [
            jnp.sum(conv_grad * extended[offset : offset + plane_rows], axis=0)
            for offset in range(3)
        ],
        axis=1,
    )
    returned = along(jnp.where(starts_here, 0.0, ext_grad[:2]), -1)
    gated_grad = ext_grad[2:] + jnp.pad(returned, ((plane_rows - 2, 0), (0, 0)))
    mixed_grad = jnp.concatenate([gated_grad * x_part, c_grad, gated_grad * b_part], axis=1)
    mixed_grad = mixed_grad.astype(LOW)
    mixed_grad, result_y, result_x = together(mixed_grad, result_y, result_x)
    result_parts = plane_settle(result_y, result_x, result_block)
    outward_y, outward_x, outward_block = plane_corner(outward_near, outward_got)
    inward_term = over_tokens(normed_one, mixed_grad).astype(LOW)
    inward_term, mixed_grad, outward_y, outward_x, down_own[0], both_own[0], *result_parts = together(
        inward_term, mixed_grad, outward_y, outward_x, down_own[0], both_own[0], *result_parts
    )
    inward_own = planes_scatter(inward_term)
    down_own += [planes_scatter(down_term)]
    block_output = (middle + sum(part.astype(F32) for part in result_parts)).astype(LOW)
    outward_parts = plane_settle(outward_y, outward_x, outward_block)
    far = against_rows(core_rows(mixed_grad, False), inward_part).astype(LOW)
    got = swap(far, "c")
    near = against_rows(core_rows(mixed_grad, True), inward_part).astype(LOW)
    got, near, both_own[1], *outward_parts = together(got, near, both_own[1], *outward_parts)
    both_got = [plane_exchange(both_own[0].reshape(8, d_rows, units))]
    outward_own = sum(part.astype(F32) for part in outward_parts).astype(LOW)
    from_y, from_x, block = plane_corner(near, got)
    from_y, from_x, both_got[0] = together(from_y, from_x, both_got[0])
    both_got += [plane_exchange(both_own[1].reshape(8, d_rows, units))]
    parts = plane_settle(from_y, from_x, block)
    *parts, both_got[1], down_own[1] = together(*parts, both_got[1], down_own[1])
    normed_one_grad = sum(part.astype(F32) for part in parts)
    scale_one, normal_one = rms_parts(inputs)
    input_grad = middle_grad + norm_back(normed_one_grad, normal_one, scale_one, gain_one)

    down_sum = jnp.concatenate(down_own, axis=0).astype(F32)

    gate_new, gate_dots = updated_ffn(both_got, 0, gate_weight, gate_first, gate_second, count)
    up_new, up_dots = updated_ffn(both_got, 1, up_weight, up_first, up_second, count)
    outward_own = planes_scatter_small(after(outward_own, parts[0]))
    inward_own, _, _, input_grad = together(inward_own, gate_new[0], up_new[0], input_grad)
    inward_own = plane_exchange(inward_own.reshape(8, d_rows, 3 * feats))
    inward_new, inward_dots = updated_inward(
        inward_own, inward_weight, inward_first, inward_second, count
    )
    own_gains = norm_gains.astype(LOW).astype(F32)
    gain_one_grad = inward_dots / own_gains[0]
    gain_two_grad = (gate_dots + up_dots) / own_gains[1]
    gains_grad = jnp.stack([gain_one_grad, gain_two_grad])
    taps_grad = sum(part.astype(F32) for part in planes_scatter_small(tap_grads)).T

    *outward_own, _ = together(*outward_own, inward_new[0])
    outward_sum = sum(part.astype(F32) for part in outward_own)
    outward_new = adamw(
        outward_weight, outward_first, outward_second, outward_sum, RATE_MATRIX, DECAY_RATE
    )
    down_new = adamw(down_weight, down_first, down_second, down_sum, RATE_MATRIX, DECAY_RATE)
    gains_new = adamw(norm_gains, gains_first, gains_second, gains_grad, RATE_VECTOR, 0.0)
    taps_new = adamw(conv_taps, taps_first, taps_second, taps_grad, RATE_VECTOR, 0.0)
    return (
        block_output,
        input_grad,
        *inward_new,
        *outward_new,
        *gate_new,
        *up_new,
        *down_new,
        *gains_new,
        *taps_new,
    )


def solution(mesh):
    devices = mesh.devices.reshape(-1, 2, 2, 2)
    rows = P(AXES, None)
    columns = P(None, AXES)
    return jax.shard_map(
        on_device,
        mesh=Mesh(devices, AXES),
        in_specs=(rows,) * 17 + (columns,) * 6,
        out_specs=(rows,) * 17 + (columns,) * 6,
        check_vma=False,
    )
```

```python
import functools

import jax
import jax.numpy as jnp
from jax import lax
from jax.experimental import pallas as pl
from jax.experimental.pallas import tpu as pltpu
from jax.sharding import Mesh
from jax.sharding import PartitionSpec as P

SEQ_BASE = 8192
STEP = 10

EPS_NORM = 1e-05
BETA_ONE = 0.9
BETA_TWO = 0.95
ADAM_EPS = 1e-08
DECAY_RATE = 0.1
RATE_MATRIX = 0.01
RATE_VECTOR = 0.3

AXES = ("p", "y", "x", "c")
PLANE = ("y", "x", "c")
LOW = jnp.bfloat16
F32 = jnp.float32


def forward_dot(operand, partner):
    return jnp.dot(operand, partner, preferred_element_type=jnp.float32)


def over_tokens(operand, partner):
    return lax.dot_general(
        operand, partner, (((0,), (0,)), ((), ())), preferred_element_type=jnp.float32
    )


def against_rows(operand, partner):
    return lax.dot_general(
        operand, partner, (((1,), (1,)), ((), ())), preferred_element_type=jnp.float32
    )


def rms_parts(values):
    scale = lax.rsqrt(jnp.mean(values * values, axis=-1, keepdims=True) + EPS_NORM)
    return (scale, values * scale)


def norm_back(upstream, normal, scale, gain):
    scaled = upstream * gain
    return scale * (scaled - normal * jnp.mean(scaled * normal, axis=-1, keepdims=True))


def adamw(weight, first, second, grad, rate, decay):
    first_new = BETA_ONE * first + (1.0 - BETA_ONE) * grad
    second_new = BETA_TWO * second + (1.0 - BETA_TWO) * grad * grad
    fix_one = 1.0 - BETA_ONE**STEP
    fix_two = 1.0 - BETA_TWO**STEP
    stepped = first_new / fix_one / (jnp.sqrt(second_new / fix_two) + ADAM_EPS)
    return (first_new, second_new, weight - rate * (stepped + decay * weight))


def after(value, *others):
    return lax.optimization_barrier((value, *others))[0]


def together(*values):
    return lax.optimization_barrier(values)


def swap(block, axis):
    return lax.ppermute(block, axis, [(0, 1), (1, 0)])


def along(block, distance):
    count = lax.axis_size("p")
    route = [(i - distance, i) for i in range(count) if 0 <= i - distance < count]
    return lax.ppermute(block, "p", route)


def over(block, axis):
    other = swap(block, axis)
    first = lax.axis_index(axis) == 0
    return jnp.stack([jnp.where(first, block, other), jnp.where(first, other, block)])


def plane_near(block):
    return block, swap(block, "x"), swap(block, "y"), swap(block, "c")


def plane_blocks(block, by_x=None, by_y=None, own_far=None):
    if by_x is None:
        block, by_x, by_y, own_far = plane_near(block)
    half = block.shape[0] // 2
    corner = jnp.concatenate([swap(by_x[:half], "y"), swap(by_y[half:], "x")], axis=0)
    near = [block, by_x, by_y, corner]
    return near, [own_far] + [swap(piece, "c") for piece in near[1:]]


def plane_gather(block, *near):
    rows = block.shape[0]
    mine_y, mine_x, mine_c = (lax.axis_index(axis) for axis in PLANE)
    out = jnp.zeros((8 * rows, block.shape[1]), block.dtype)
    for dc, pieces in enumerate(plane_blocks(block, *near)):
        for k, piece in enumerate(pieces):
            at = ((mine_y ^ (k >> 1)) * 2 + (mine_x ^ (k & 1))) * 2 + (mine_c ^ dc)
            out = lax.dynamic_update_slice_in_dim(out, piece, at * rows, axis=0)
    return out


def plane_gather_here(block):
    near, far = plane_blocks(block)
    return jnp.concatenate(near + far, axis=0)


def plane_exchange(blocks):
    return lax.all_to_all(blocks, PLANE, split_axis=0, concat_axis=0, tiled=True)


def core_rows(array, own):
    core = lax.axis_index("c") if own else 1 - lax.axis_index("c")
    rows = array.shape[0] // 8
    return jnp.concatenate(
        [lax.dynamic_slice_in_dim(array, (2 * i + core) * rows, rows, axis=0) for i in range(4)],
        axis=0,
    )


def plane_corner(near, got, here=False):
    quarter = near.shape[0] // 4
    half = quarter // 2
    mine_y, mine_x = lax.axis_index("y"), lax.axis_index("x")

    def block(dy, dx):
        if here:
            place = 2 * dy + dx
            return tuple(part[place * quarter : (place + 1) * quarter] for part in (near, got))
        place = (mine_y ^ dy) * 2 + (mine_x ^ dx)
        return tuple(
            lax.dynamic_slice_in_dim(part, place * quarter, quarter, axis=0) for part in (near, got)
        )

    corner = sum(block(1, 1))
    return swap(corner[:half], "y"), swap(corner[half:], "x"), block


def plane_settle(from_y, from_x, block):
    near_x, got_x = block(0, 1)
    near_y, got_y = block(1, 0)
    by_x = near_x + got_x + jnp.concatenate([from_y, jnp.zeros_like(from_y)], axis=0)
    by_y = near_y + got_y + jnp.concatenate([jnp.zeros_like(from_x), from_x], axis=0)
    return sum(block(0, 0)), swap(by_x, "x"), swap(by_y, "y")


def planes_gather(block):
    return lax.all_gather(block, "p", axis=0, tiled=True)


def planes_scatter(term):
    return lax.psum_scatter(term, "p", scatter_dimension=0, tiled=True)


def shifted(block, distance):
    count = lax.axis_size("p")
    return lax.ppermute(block, "p", [((i + distance) % count, i) for i in range(count)])


def planes_scatter_small(term):
    count = lax.axis_size("p")
    if count > 4:
        return [planes_scatter(term)]
    rows = term.shape[0] // count
    mine = lax.axis_index("p")
    parts = [lax.dynamic_slice_in_dim(term, mine * rows, rows, axis=0)]
    for i in range(1, count):
        piece = lax.dynamic_slice_in_dim(term, (mine - i) % count * rows, rows, axis=0)
        parts.append(shifted(piece, i))
    return parts


def half_body(rows_ref, upstream_ref, both_ref, down_ref, hidden_out, grads_out):
    both = forward_dot(rows_ref[...], both_ref[...])
    half = both.shape[1] // 2
    gate_value, up_value = both[:, :half], both[:, half:]
    sigmoid_gate = jax.nn.sigmoid(gate_value)
    silu_gate = gate_value * sigmoid_gate
    hidden_out[...] = (silu_gate * up_value).astype(LOW)
    hidden_grad = against_rows(upstream_ref[...], down_ref[...])
    gate_grad = hidden_grad * up_value * sigmoid_gate * (1.0 + gate_value * (1.0 - sigmoid_gate))
    grads_out[:, :half] = gate_grad.astype(LOW)
    grads_out[:, half:] = (hidden_grad * silu_gate).astype(LOW)


def half_ffn(rows, upstream, both, down):
    count, d = rows.shape
    half = both.shape[1] // 2
    tile = 512
    return pl.pallas_call(
        half_body,
        grid=(count // tile,),
        in_specs=[
            pl.BlockSpec((tile, d), lambda i: (i, 0)),
            pl.BlockSpec((tile, d), lambda i: (i, 0)),
            pl.BlockSpec(both.shape, lambda i: (0, 0)),
            pl.BlockSpec(down.shape, lambda i: (0, 0)),
        ],
        out_specs=[
            pl.BlockSpec((tile, half), lambda i: (i, 0)),
            pl.BlockSpec((tile, 2 * half), lambda i: (i, 0)),
        ],
        out_shape=[
            jax.ShapeDtypeStruct((count, half), LOW),
            jax.ShapeDtypeStruct((count, 2 * half), LOW),
        ],
        compiler_params=pltpu.CompilerParams(vmem_limit_bytes=48 * 2**20),
        cost_estimate=pl.CostEstimate(
            flops=6 * count * d * half, transcendentals=count * half, bytes_accessed=4 * count * d + 6 * d * half
        ),
    )(rows, upstream, both, down)


def pair_body(turned, a_ref, b_ref, c_ref, e_ref, out_ref):
    dot = against_rows if turned else forward_dot
    out_ref[...] = (dot(a_ref[...], c_ref[...]) + dot(b_ref[...], e_ref[...])).astype(LOW)


def pair_dot(first, second, first_weight, second_weight, far, turned):
    count, depth = first.shape
    width = first_weight.shape[0 if turned else 1]
    tile = 512
    steps = count // 2 // tile
    rows = pl.BlockSpec((tile, depth), lambda i: (i + (steps if far else 0), 0))
    whole = pl.BlockSpec(first_weight.shape, lambda i: (0, 0))
    return pl.pallas_call(
        functools.partial(pair_body, turned),
        grid=(steps,),
        in_specs=[rows, rows, whole, whole],
        out_specs=pl.BlockSpec((tile, width), lambda i: (i, 0)),
        out_shape=jax.ShapeDtypeStruct((count // 2, width), LOW),
        compiler_params=pltpu.CompilerParams(vmem_limit_bytes=48 * 2**20),
        cost_estimate=pl.CostEstimate(
            flops=2 * count * depth * width, transcendentals=0, bytes_accessed=2 * count * (depth + width // 2) + 4 * depth * width
        ),
    )(first, second, first_weight, second_weight)


def pack_body(count, inward_ref, gate_ref, up_ref, inward_out, ffn_out):
    d_rows = inward_ref.shape[1] // (24 * count)
    ff_rows = gate_ref.shape[1] // (8 * count)
    feats, units, width = count * d_rows, count * ff_rows, ff_rows // 2
    for p in range(count):
        for to in range(8):
            at = (p * 8 + to) * ff_rows
            for half in range(2):
                for kind, ref in enumerate((gate_ref, up_ref)):
                    lane = (half * 2 + kind) * units // 2 + p * width
                    block = ref[:, at + half * width : at + (half + 1) * width]
                    ffn_out[to, :, lane : lane + width] = block.astype(LOW)
    for part in range(3):
        for to in range(8):
            blocks = []
            for p in range(count):
                at = ((part * count + p) * 8 + to) * d_rows
                blocks.append(inward_ref[:, at : at + d_rows])
            block = jnp.concatenate(blocks, axis=1).astype(LOW)
            inward_out[to, :, part * feats : (part + 1) * feats] = block


def packed(inward, gate, up, count):
    d_rows, ff = gate.shape
    feats, units = inward.shape[1] // 24, ff // 8
    if d_rows % 64 or units % (256 * count):
        sent = inward.astype(LOW).reshape(d_rows, 3, count, 8, -1)
        sent = sent.transpose(3, 0, 1, 2, 4).reshape(8, d_rows, 3 * feats)
        both = jnp.stack([gate.astype(LOW), up.astype(LOW)], axis=1)
        both = both.reshape(d_rows, 2, count, 8, 2, -1).transpose(3, 0, 4, 1, 2, 5)
        return sent, both.reshape(8, d_rows, 2 * units)
    rows = 16
    return pl.pallas_call(
        functools.partial(pack_body, count),
        grid=(d_rows // rows,),
        in_specs=[
            pl.BlockSpec((rows, 24 * feats), lambda i: (i, 0)),
            pl.BlockSpec((rows, ff), lambda i: (i, 0)),
            pl.BlockSpec((rows, ff), lambda i: (i, 0)),
        ],
        out_specs=[
            pl.BlockSpec((8, rows, 3 * feats), lambda i: (0, i, 0)),
            pl.BlockSpec((8, rows, 2 * units), lambda i: (0, i, 0)),
        ],
        out_shape=[
            jax.ShapeDtypeStruct((8, d_rows, 3 * feats), LOW),
            jax.ShapeDtypeStruct((8, d_rows, 2 * units), LOW),
        ],
        compiler_params=pltpu.CompilerParams(vmem_limit_bytes=32 * 2**20),
        cost_estimate=pl.CostEstimate(
            flops=0, transcendentals=0, bytes_accessed=6 * d_rows * (24 * feats + 2 * ff)
        ),
    )(inward, gate, up)


def update_body(parts, width, pieces, *refs):
    got_refs = refs[:parts]
    weight_ref, first_ref, second_ref, first_out, second_out, weight_out, dot_out = refs[parts:]

    @pl.when(pl.program_id(0) == 0)
    def _():
        dot_out[...] = jnp.zeros_like(dot_out)

    total = jnp.zeros((weight_ref.shape[0], 128), F32)
    joined = 128 // width
    for group in range(0, len(pieces), joined):
        grad = [
            got_refs[which][tuple(at)][:, lane : lane + width].astype(F32)
            for which, *at, lane in pieces[group : group + joined]
        ]
        grad = jnp.concatenate(grad, axis=1) if joined > 1 else grad[0]
        here = slice(group * width, group * width + 128)
        weight = weight_ref[:, here]
        first, second, updated = adamw(
            weight, first_ref[:, here], second_ref[:, here], grad, RATE_MATRIX, DECAY_RATE
        )
        first_out[:, here] = first
        second_out[:, here] = second
        weight_out[:, here] = updated
        total += weight.astype(LOW).astype(F32) * grad
    dot_out[...] += total


def update_call(grid, got, got_specs, width, pieces, weight, first, second):
    rows, columns = weight.shape
    spec = pl.BlockSpec((rows, columns // grid), lambda k: (0, k))
    shape = jax.ShapeDtypeStruct(weight.shape, F32)
    *new, dots = pl.pallas_call(
        functools.partial(update_body, len(got), width, pieces),
        grid=(grid,),
        in_specs=[*got_specs, spec, spec, spec],
        out_specs=[spec, spec, spec, pl.BlockSpec((rows, 128), lambda k: (0, 0))],
        out_shape=[shape, shape, shape, jax.ShapeDtypeStruct((rows, 128), F32)],
        compiler_params=pltpu.CompilerParams(vmem_limit_bytes=32 * 2**20),
        cost_estimate=pl.CostEstimate(
            flops=20 * rows * columns, transcendentals=2 * rows * columns, bytes_accessed=26 * rows * columns
        ),
    )(*got, weight, first, second)
    return tuple(new), jnp.sum(dots, axis=1)


def updated_plainly(grad, weight, first, second):
    grad = grad.reshape(weight.shape).astype(F32)
    new = adamw(weight, first, second, grad, RATE_MATRIX, DECAY_RATE)
    return new, jnp.sum(weight.astype(LOW).astype(F32) * grad, axis=1)


def updated_inward(got, weight, first, second, count):
    rows, columns = weight.shape
    width = columns // (24 * count)
    if width % 64 or rows % 16:
        grad = got.reshape(8, rows, 3, count, width).transpose(1, 2, 3, 0, 4)
        return updated_plainly(grad, weight, first, second)
    spec = pl.BlockSpec((8, rows, count * width), lambda k: (0, 0, k))
    pieces = [(0, to, p * width) for p in range(count) for to in range(8)]
    return update_call(3, [got], [spec], width, pieces, weight, first, second)


def updated_ffn(got, kind, weight, first, second, count):
    rows, columns = weight.shape
    width = columns // (16 * count)
    if width % 128 or rows % 16:
        grad = jnp.stack(got).reshape(2, 8, rows, 2, count, width)[:, :, :, kind]
        return updated_plainly(grad.transpose(2, 3, 1, 0, 4), weight, first, second)
    spec = pl.BlockSpec((4, rows, width), lambda k: (k % 2, 0, kind * count + k // 2))
    pieces = [
        (half, q, lane) for q in range(4) for half in range(2) for lane in range(0, width, 128)
    ]
    return update_call(2 * count, got, [spec, spec], 128, pieces, weight, first, second)


def on_device(
    block_input,
    cotangent,
    inward_weight,
    inward_first,
    inward_second,
    outward_weight,
    outward_first,
    outward_second,
    gate_weight,
    gate_first,
    gate_second,
    up_weight,
    up_first,
    up_second,
    down_weight,
    down_first,
    down_second,
    norm_gains,
    gains_first,
    gains_second,
    conv_taps,
    taps_first,
    taps_second,
):
    count = lax.axis_size("p")
    tok_rows, d = block_input.shape
    d_rows = inward_weight.shape[0]
    ff = gate_weight.shape[1]
    ff_rows = down_weight.shape[0]
    plane_rows = 8 * tok_rows
    near_rows = 4 * tok_rows
    seq_len = min(SEQ_BASE, plane_rows * count)
    feats = d // 8
    units = ff // 8
    half = units // 2
    place = lax.axis_index(PLANE)

    down_low = down_weight.astype(LOW)
    down_a, down_b = down_low[: ff_rows // 2], down_low[ff_rows // 2 :]
    small = jnp.concatenate([norm_gains, conv_taps], axis=0).astype(LOW)
    small = jnp.pad(small, ((0, 11), (0, d - d_rows)))
    first = jnp.concatenate([down_a, outward_weight.astype(LOW), small], axis=0)
    first_part = planes_gather(first)
    block_here, inward_here, _ = together(block_input, inward_weight, first)
    inward_sent, ffn_sent = packed(inward_here, gate_weight, up_weight, count)
    inward_got = plane_exchange(inward_sent).reshape(8 * d_rows, 3 * feats)
    ffn_got = plane_exchange(after(ffn_sent, inward_got)).reshape(8 * d_rows, 2 * units)
    *inputs_near, inward_got, ffn_got, first_part = together(
        *plane_near(block_here), inward_got, ffn_got, first_part
    )
    inward_part = planes_gather(inward_got)
    ffn_parts = [planes_gather(ffn_got[:, :units]), planes_gather(ffn_got[:, units:])]
    first_part = first_part.reshape(count, -1, d)
    down_parts = [first_part[:, : ff_rows // 2].reshape(-1, d), planes_gather(down_b)]
    outward_part = first_part[:, ff_rows // 2 : ff_rows // 2 + d_rows].reshape(-1, d)
    small = first_part[:, ff_rows // 2 + d_rows :][:, :5, :d_rows]
    small = over(over(over(small, "c"), "x"), "y").transpose(3, 0, 1, 2, 4, 5)
    inputs_low = plane_gather(*inputs_near)
    inputs_low, small, outward_part = together(inputs_low, small, outward_part)
    outward_full = plane_gather(outward_part)
    small = small.astype(F32)
    gain_one = small[..., 0, :].reshape(d)
    gain_two = small[..., 1, :].reshape(d)
    taps_here = lax.dynamic_index_in_dim(
        small.reshape(count, 8, 5, d_rows), place, axis=1, keepdims=False
    )
    taps_here = taps_here[:, 2:].transpose(1, 0, 2).reshape(3, feats)
    tap_zero, tap_one, tap_two = taps_here[0], taps_here[1], taps_here[2]

    _, normed_one = rms_parts(inputs_low.astype(F32))
    normed_one = (normed_one * gain_one).astype(LOW)
    mixed = forward_dot(normed_one, inward_part)
    mixed, cotangent_here = together(mixed, cotangent)
    upstream = plane_gather_here(cotangent_here)
    b_part = mixed[:, :feats]
    c_part = mixed[:, feats : 2 * feats]
    x_part = mixed[:, 2 * feats :]
    gated = b_part * x_part
    starts_here = lax.axis_index("p") * plane_rows % seq_len == 0
    before = jnp.where(starts_here, 0.0, along(gated[plane_rows - 2 :], 1))
    extended = jnp.concatenate([before, gated], axis=0)
    convolved = (
        tap_zero * extended[:plane_rows]
        + tap_one * extended[1 : plane_rows + 1]
        + tap_two * extended[2:]
    )
    branch_feats = (c_part * convolved).astype(LOW)
    branch_got = plane_exchange(branch_feats.reshape(8, tok_rows, feats))
    branch_in = branch_got.transpose(1, 0, 2).reshape(tok_rows, d)
    branch_in, upstream = together(branch_in, upstream)
    inputs = block_input.astype(F32)
    middle = inputs + forward_dot(branch_in, outward_full)
    scale_two, normal_two = rms_parts(middle)
    normed_two = plane_gather_here((normal_two * gain_two).astype(LOW))

    def terms_of(hidden, grads):
        return over_tokens(hidden, upstream).astype(LOW), over_tokens(normed_two, grads).astype(LOW)

    hidden_a, grads_a = half_ffn(normed_two, upstream, ffn_parts[0], down_parts[0])
    down_term, both_term = terms_of(hidden_a, grads_a)
    down_own, both_own = [planes_scatter(down_term)], [planes_scatter(both_term)]
    ffn_b, down_b, _, _ = together(ffn_parts[1], down_parts[1], down_term, both_term)
    hidden_b, grads_b = half_ffn(normed_two, upstream, ffn_b, down_b)
    far = pair_dot(grads_a, grads_b, ffn_parts[0], ffn_b, True, True)
    got = swap(far, "c")
    near = pair_dot(grads_a, grads_b, ffn_parts[0], ffn_b, False, True)
    got, near, hidden_b, grads_b = together(got, near, hidden_b, grads_b)
    from_y, from_x, block = plane_corner(near, got, True)
    both_term = over_tokens(normed_two, grads_b).astype(LOW)
    from_y, from_x, both_term = together(from_y, from_x, both_term)
    both_own += [planes_scatter(both_term)]
    down_term = over_tokens(hidden_b, upstream).astype(LOW)
    result_far = pair_dot(hidden_a, hidden_b, down_parts[0], down_b, True, False)
    result_near = pair_dot(hidden_a, hidden_b, down_parts[0], down_b, False, False)
    *parts, down_term, result_far, result_near = together(
        *plane_settle(from_y, from_x, block), down_term, result_far, result_near
    )
    normed_two_grad = sum(part.astype(F32) for part in parts)

    result_got = swap(result_far, "c")
    middle_grad = cotangent.astype(F32) + norm_back(
        normed_two_grad, normal_two, scale_two, gain_two
    )
    branch_grad = middle_grad.astype(LOW)
    branch_in_grad = against_rows(branch_grad, outward_full).astype(LOW)

    def outward_rows(own):
        core = lax.axis_index("c") if own else 1 - lax.axis_index("c")
        split = branch_got.reshape(4, 2, tok_rows, feats)
        part = lax.dynamic_index_in_dim(split, core, axis=1, keepdims=False)
        term = lax.dot_general(
            part, branch_grad, (((1,), (0,)), ((), ())), preferred_element_type=jnp.float32
        )
        return term.astype(LOW).reshape(d // 2, d)

    outward_far = outward_rows(False)
    branch_in_grad, result_got, result_near, outward_far = together(
        branch_in_grad, result_got, result_near, outward_far
    )
    branch_in_grad = plane_exchange(branch_in_grad.reshape(tok_rows, 8, feats).transpose(1, 0, 2))
    result_y, result_x, result_block = plane_corner(result_near, result_got, True)
    outward_got, outward_near = swap(outward_far, "c"), outward_rows(True)
    branch_in_grad, outward_got, outward_near, down_own[0], both_own[0] = together(
        branch_in_grad, outward_got, outward_near, down_own[0], both_own[0]
    )
    branch_in_grad = branch_in_grad.reshape(plane_rows, feats).astype(F32)
    c_grad = branch_in_grad * convolved
    conv_grad = branch_in_grad * c_part
    ext_grad = (
        jnp.pad(tap_zero * conv_grad, ((0, 2), (0, 0)))
        + jnp.pad(tap_one * conv_grad, ((1, 1), (0, 0)))
        + jnp.pad(tap_two * conv_grad, ((2, 0), (0, 0)))
    )
    tap_grads = jnp.stack(
        [
            jnp.sum(conv_grad * extended[offset : offset + plane_rows], axis=0)
            for offset in range(3)
        ],
        axis=1,
    )
    returned = along(jnp.where(starts_here, 0.0, ext_grad[:2]), -1)
    gated_grad = ext_grad[2:] + jnp.pad(returned, ((plane_rows - 2, 0), (0, 0)))
    mixed_grad = jnp.concatenate([gated_grad * x_part, c_grad, gated_grad * b_part], axis=1)
    mixed_grad = mixed_grad.astype(LOW)
    mixed_grad, result_y, result_x = together(mixed_grad, result_y, result_x)
    result_parts = plane_settle(result_y, result_x, result_block)
    outward_y, outward_x, outward_block = plane_corner(outward_near, outward_got)
    inward_term = over_tokens(normed_one, mixed_grad).astype(LOW)
    both_got = [plane_exchange(both_own[0].reshape(8, d_rows, units))]
    inward_term, mixed_grad, outward_y, outward_x, both_own[1], both_got[0], *result_parts = together(
        inward_term, mixed_grad, outward_y, outward_x, both_own[1], both_got[0], *result_parts
    )
    inward_own = planes_scatter(inward_term)
    block_output = (middle + sum(part.astype(F32) for part in result_parts)).astype(LOW)
    outward_parts = plane_settle(outward_y, outward_x, outward_block)
    far = against_rows(core_rows(mixed_grad, False), inward_part).astype(LOW)
    got = swap(far, "c")
    near = against_rows(core_rows(mixed_grad, True), inward_part).astype(LOW)
    both_got += [plane_exchange(both_own[1].reshape(8, d_rows, units))]
    got, near, down_term, *outward_parts = together(got, near, down_term, *outward_parts)
    down_own += [planes_scatter(down_term)]
    outward_own = sum(part.astype(F32) for part in outward_parts).astype(LOW)
    from_y, from_x, block = plane_corner(near, got)
    from_y, from_x, both_got[1] = together(from_y, from_x, both_got[1])

    gate_new, gate_dots = updated_ffn(both_got, 0, gate_weight, gate_first, gate_second, count)
    up_new, up_dots = updated_ffn(both_got, 1, up_weight, up_first, up_second, count)
    inward_own = plane_exchange(inward_own.reshape(8, d_rows, 3 * feats))
    outward_own = planes_scatter_small(outward_own)
    *parts, inward_own, gate_dots, up_dots = together(
        *plane_settle(from_y, from_x, block), inward_own, gate_dots, up_dots
    )
    normed_one_grad = sum(part.astype(F32) for part in parts)
    scale_one, normal_one = rms_parts(inputs)
    input_grad = middle_grad + norm_back(normed_one_grad, normal_one, scale_one, gain_one)
    down_sum = jnp.concatenate(down_own, axis=0).astype(F32)
    inward_new, inward_dots = updated_inward(
        inward_own, inward_weight, inward_first, inward_second, count
    )
    own_gains = norm_gains.astype(LOW).astype(F32)
    gain_one_grad = inward_dots / own_gains[0]
    gain_two_grad = (gate_dots + up_dots) / own_gains[1]
    gains_grad = jnp.stack([gain_one_grad, gain_two_grad])
    taps_grad = sum(part.astype(F32) for part in planes_scatter_small(tap_grads)).T

    *outward_own, _ = together(*outward_own, inward_new[0])
    outward_sum = sum(part.astype(F32) for part in outward_own)
    outward_new = adamw(
        outward_weight, outward_first, outward_second, outward_sum, RATE_MATRIX, DECAY_RATE
    )
    down_new = adamw(down_weight, down_first, down_second, down_sum, RATE_MATRIX, DECAY_RATE)
    gains_new = adamw(norm_gains, gains_first, gains_second, gains_grad, RATE_VECTOR, 0.0)
    taps_new = adamw(conv_taps, taps_first, taps_second, taps_grad, RATE_VECTOR, 0.0)
    return (
        block_output,
        input_grad,
        *inward_new,
        *outward_new,
        *gate_new,
        *up_new,
        *down_new,
        *gains_new,
        *taps_new,
    )


def solution(mesh):
    devices = mesh.devices.reshape(-1, 2, 2, 2)
    rows = P(AXES, None)
    columns = P(None, AXES)
    return jax.shard_map(
        on_device,
        mesh=Mesh(devices, AXES),
        in_specs=(rows,) * 17 + (columns,) * 6,
        out_specs=(rows,) * 17 + (columns,) * 6,
        check_vma=False,
    )
```
